128 devices in a mesh: wide: 16 (over z, y), narrow: 8 (over x, core).
Axes of the slice: x: 4, y: 4, z: 4, core: 2. Of those that a mesh axis runs over, the one named last changes fastest.
Arguments:
- points: float32 [6, 1048576], P(None, ('wide', 'narrow')), may hold values from -6 to 6
- charges: float32 [16, 1048576], P(None, ('wide', 'narrow')), may hold values from -6 to 6
- leaf_skel: float32 [6, 524288], P(None, ('wide', 'narrow')), may hold values from -6 to 6
- node_skel: float32 [6, 8192], replicated, may hold values from -6 to 6
- group_skel: float32 [6, 1024], replicated, may hold values from -6 to 6
- source_basis: float32 [8192, 64, 128], P(('wide', 'narrow')), may hold values from -0.5 to 0.5
- target_basis: float32 [8192, 64, 128], P(('wide', 'narrow')), may hold values from -0.75 to 0.75
- leaf_upward: float32 [64, 524288], P(None, ('wide', 'narrow')), may hold values from -0.09375 to 0.09375
- leaf_downward: float32 [64, 524288], P(None, ('wide', 'narrow')), may hold values from -0.75 to 0.75
- node_upward: float32 [64, 8192], replicated, may hold values from -0.25 to 0.25
- node_downward: float32 [64, 8192], P(None, ('wide', 'narrow')), may hold values from -0.75 to 0.75
- near_list: int32 [8192, 8], P(('wide', 'narrow')), may hold values from -1 to 8191, as said below
- leaf_links: int32 [8192, 8], P(('wide', 'narrow')), may hold values from -1 to 8191, as said below
- node_links: int32 [128, 4], P(('wide', 'narrow')), may hold values from -1 to 127, as said below
- group_links: int32 [16, 8], P('wide'), may hold values from -1 to 15, as said below
Outputs:
- potential: float32 [16, 1048576], P(None, ('wide', 'narrow'))
The draws below stay inside these ranges and needn't reach their ends.
Inputs may be any that keep to these rules, and one draw needn't show every extreme that they name: `near_list`: entry 0 of row l is l; the other used entries are distinct leaf clusters other than l within 64 of l; one device's rows hold at most 288 used entries together, exactly so many on every device but the first and the last. `leaf_links`: used entries of row l are distinct leaf clusters within 64 of l, none equal to l or to an entry of near_list row l. `node_links`: used entries of row d are distinct other nodes of the same group of 8 nodes. `group_links`: used entries of row g are distinct other groups.
All inputs are finite; a program needn't handle non-finite values.
Results may differ from the reference program's by a relative error of at most 0.0003.
Values sent between devices are 32-bit elements; how exact they have to be, the bound alone decides.
A program may use at most 64 MiB of HBM per device.

```python
import math
import jax
import jax.numpy as jnp
from jax import lax

LEAF = 128
RANK = 64
RHS = 16
CL_DEV = 64
NEAR = 8
FAR = 8
DFAR = 4
GFAR = 8
HALO = 64
GROUP = 8
NODES = 128
NL = 8192
NP = 1048576
N_WIDE = 16


def link_tables(key):
    first_key = jax.random.fold_in(key, 11)
    second_key = jax.random.fold_in(key, 12)
    width = 2 * HALO
    slots = jnp.arange(width, dtype=jnp.int32)
    steps_away = jnp.where(slots < HALO, slots - HALO, slots - HALO + 1)
    scores = jax.random.randint(first_key, (NL, width), 0, 1 << 20) * width + slots[None, :]
    ranking = jnp.argsort(scores, axis=1)
    offsets = steps_away[ranking]
    member = jnp.arange(CL_DEV, dtype=jnp.int32)
    count_scores = jax.random.randint(second_key, (NODES, CL_DEV), 0, 1 << 20) * CL_DEV + member[None, :]
    count_rank = jnp.argsort(count_scores, axis=1).astype(jnp.int32)
    counts = (1 + count_rank % NEAR).reshape(NL)
    leaf_index = jnp.arange(NL, dtype=jnp.int32)[:, None]
    near_cands = leaf_index + offsets[:, :NEAR - 1]
    near_slot = jnp.arange(1, NEAR, dtype=jnp.int32)[None, :]
    near_good = (near_slot < counts[:, None]) & (near_cands >= 0) & (near_cands < NL)
    near_rest = jnp.where(near_good, near_cands, -1)
    near_table = jnp.concatenate([leaf_index, near_rest], axis=1).astype(jnp.int32)
    far_cands = leaf_index + offsets[:, NEAR - 1:NEAR - 1 + FAR]
    far_table = jnp.where((far_cands >= 0) & (far_cands < NL), far_cands, -1).astype(jnp.int32)
    return (near_table, far_table)


def draw_near_list(key, part):
    return link_tables(key)[0]


def draw_leaf_links(key, part):
    return link_tables(key)[1]


def member_links(key, rows, members, picks):
    span = max(picks, members)
    places = jnp.arange(span, dtype=jnp.int32)
    row_index = jnp.arange(rows, dtype=jnp.int32)
    inside = row_index % members
    random_part = jax.random.randint(key, (rows, span), 0, 1 << 20) * span + places[None, :]
    is_self = places[None, :] == inside[:, None]
    is_padding = places[None, :] >= members
    scores = jnp.where(is_self, (1 << 20) * span + 1, random_part)
    scores = jnp.where(is_padding, (1 << 20) * span + 2 + places[None, :], scores)
    ranking = jnp.argsort(scores, axis=1)[:, :picks].astype(jnp.int32)
    good = (ranking < members) & (ranking != inside[:, None])
    chosen = (row_index // members)[:, None] * members + ranking
    return jnp.where(good, chosen, -1).astype(jnp.int32)


def draw_node_links(key, part):
    return member_links(jax.random.fold_in(key, 21), NODES, GROUP, DFAR)


def draw_group_links(key, part):
    return member_links(jax.random.fold_in(key, 31), N_WIDE, N_WIDE, GFAR)


def block_scale(rng, dims, shards, least, high):
    factor_of = 1.0
    for axis_at, parts in shards:
        heights = jax.random.uniform(jax.random.fold_in(jax.random.fold_in(rng, 6), axis_at), (parts,), jnp.float32, least / len(shards), high / len(shards))
        factor_of = factor_of * jnp.repeat(jnp.exp(heights), dims[axis_at] // parts).reshape((-1,) + (1,) * (len(dims) - 1 - axis_at))
    return factor_of


def centred(key, dims, spread, most, cuts=(), kind=jnp.bfloat16):
    gain = block_scale(key, dims, cuts, -0.22, 0.18) if cuts else 1.0
    drawn = jax.random.normal(key, dims, jnp.float32) * spread * gain
    return jnp.minimum(jnp.maximum(drawn, -most), most).astype(kind)


def setup_inputs(seed: int = 0) -> dict:
    arg_keys = jax.random.split(jax.random.key(seed), 16)
    return {
        "points": centred(arg_keys[0], (6, NP), 1.0, 6.0, ((1, 128),), jnp.float32),
        "charges": centred(arg_keys[1], (RHS, NP), 1.0, 6.0, ((1, 128),), jnp.float32),
        "leaf_skel": centred(arg_keys[2], (6, NL * RANK), 1.0, 6.0, ((1, 128),), jnp.float32),
        "node_skel": centred(arg_keys[3], (6, NODES * RANK), 1.0, 6.0, (), jnp.float32),
        "group_skel": centred(arg_keys[4], (6, N_WIDE * RANK), 1.0, 6.0, (), jnp.float32),
        "source_basis": centred(arg_keys[5], (NL, RANK, LEAF), LEAF ** -0.5, 0.5, ((0, 128),), jnp.float32),
        "target_basis": centred(arg_keys[6], (NL, RANK, LEAF), RANK ** -0.5, 0.75, ((0, 128),), jnp.float32),
        "leaf_upward": centred(arg_keys[7], (RANK, NL * RANK), (CL_DEV * RANK) ** -0.5, 0.09375, ((1, 128),), jnp.float32),
        "leaf_downward": centred(arg_keys[8], (RANK, NL * RANK), RANK ** -0.5, 0.75, ((1, 128),), jnp.float32),
        "node_upward": centred(arg_keys[9], (RANK, NODES * RANK), (GROUP * RANK) ** -0.5, 0.25, (), jnp.float32),
        "node_downward": centred(arg_keys[10], (RANK, NODES * RANK), RANK ** -0.5, 0.75, ((1, 128),), jnp.float32),
        "near_list": draw_near_list(jax.random.fold_in(arg_keys[15], 71), 0),
        "leaf_links": draw_leaf_links(jax.random.fold_in(arg_keys[15], 71), 0),
        "node_links": draw_node_links(jax.random.fold_in(arg_keys[15], 71), 0),
        "group_links": draw_group_links(jax.random.fold_in(arg_keys[15], 71), 0),
    }


PRECISE = lax.Precision.HIGHEST
SMOOTH = 0.25
COEFFICIENT = 1.0 / (4.0 * math.pi)

def double_layer(targets, sources):
    offset = targets[..., :, None] - sources[:3][..., None, :]
    distance = lax.optimization_barrier(jnp.sum(offset * offset, axis=0)) + SMOOTH
    flux_term = lax.optimization_barrier(jnp.sum(offset * sources[3:6][..., None, :], axis=0))
    return flux_term * lax.rsqrt(distance) / distance * COEFFICIENT

def couple(target_points, source_points, source_values, links):
    usable = (links >= 0).astype(jnp.float32)
    picked = jnp.maximum(links, 0)
    sources = source_points[:, picked]
    count = links.shape[1]
    targets = jnp.broadcast_to(target_points[:, :, None, :], (3, target_points.shape[1], count, target_points.shape[2]))
    kernel = double_layer(targets, sources)
    weights = source_values[:, picked] * usable[None, :, :, None]
    return jnp.einsum('qmfs,mfts->qmt', weights, kernel, precision=PRECISE)

def reference(points, charges, leaf_skel, node_skel, group_skel, source_basis, target_basis, leaf_upward, leaf_downward, node_upward, node_downward, near_list, leaf_links, node_links, group_links):
    point_cube = points.reshape(6, NL, LEAF)
    charge_cube = charges.reshape(RHS, NL, LEAF)

    def near_block(start):
        leaf_ids = start + jnp.arange(8, dtype=jnp.int32)
        entries = near_list[leaf_ids]
        usable = (entries >= 0).astype(jnp.float32)
        picked = jnp.maximum(entries, 0)
        sources = point_cube[:, picked]
        targets = jnp.broadcast_to(point_cube[:3, leaf_ids][:, :, None, :], (3, 8, NEAR, LEAF))
        kernel = double_layer(targets, sources)
        weights = charge_cube[:, picked] * usable[None, :, :, None]
        return jnp.einsum('qbns,bnts->qbt', weights, kernel, precision=PRECISE)
    starts = jnp.arange(NL // 8, dtype=jnp.int32) * 8
    near_part = lax.map(near_block, starts)
    near_part = jnp.transpose(near_part, (1, 0, 2, 3)).reshape(RHS, NP)
    leaf_charges = jnp.einsum('qlp,lrp->qlr', charge_cube, source_basis, precision=PRECISE)
    node_charges = jnp.einsum('rdk,qdk->qdr', leaf_upward.reshape(RANK, NODES, CL_DEV * RANK), leaf_charges.reshape(RHS, NODES, CL_DEV * RANK), precision=PRECISE)
    group_charges = jnp.einsum('rgdk,qgdk->qgr', node_upward.reshape(RANK, N_WIDE, GROUP, RANK), node_charges.reshape(RHS, N_WIDE, GROUP, RANK), precision=PRECISE)
    group_cube = group_skel.reshape(6, N_WIDE, RANK)
    group_fields = couple(group_cube[:3], group_cube, group_charges, group_links)
    node_cube = node_skel.reshape(6, NODES, RANK)
    node_fields = jnp.einsum('qdr,rdk->qdk', jnp.repeat(group_fields, GROUP, axis=1), node_downward.reshape(RANK, NODES, RANK), precision=PRECISE)
    node_fields = node_fields + couple(node_cube[:3], node_cube, node_charges, node_links)
    leaf_cube = leaf_skel.reshape(6, NL, RANK)

    def far_block(start):
        leaf_ids = start + jnp.arange(8, dtype=jnp.int32)
        return couple(leaf_cube[:3, leaf_ids], leaf_cube, leaf_charges, leaf_links[leaf_ids])
    leaf_couple = lax.map(far_block, starts)
    leaf_couple = jnp.transpose(leaf_couple, (1, 0, 2, 3)).reshape(RHS, NL, RANK)
    leaf_fields = jnp.einsum('qlr,rlk->qlk', jnp.repeat(node_fields, CL_DEV, axis=1), leaf_downward.reshape(RANK, NL, RANK), precision=PRECISE)
    leaf_fields = leaf_fields + leaf_couple
    far_part = jnp.einsum('qlr,lrp->qlp', leaf_fields, target_basis, precision=PRECISE).reshape(RHS, NP)
    return near_part + far_part
```

```python
import functools
import math

import jax
import jax.numpy as jnp
from jax import lax
from jax.experimental import pallas as pl
from jax.experimental.pallas import tpu as pltpu
from jax.sharding import PartitionSpec as P

MESH = pl.DeviceIdType.MESH
HIGH = lax.Precision.HIGHEST
F32, BF16 = jnp.float32, jnp.bfloat16
SMOOTH = 0.25
COEFFICIENT = 1.0 / (4.0 * math.pi)
NT = (((1,), (1,)), ((), ()))
NN = (((1,), (0,)), ((), ()))
NEAR_PAIRS = 288
NEAR_STEP = 16
VMEM_LIMIT = 56 * 2**20


def dot(a, b, dims, precision=None):
    return lax.dot_general(a, b, dims, precision=precision, preferred_element_type=F32)


def halves(x):
    high = x.astype(BF16)
    return high, (x - high.astype(F32)).astype(BF16)


def twice(x):
    high, low = halves(x)
    stacked = jnp.concatenate([high, low], axis=0)
    return jnp.concatenate([stacked, stacked], axis=1)


def beside(x):
    high, low = halves(x)
    return jnp.concatenate([high, low], axis=1)


def pieces(x):
    first = x.astype(BF16).astype(F32)
    rest = x - first
    second = rest.astype(BF16).astype(F32)
    return first, second, rest - second


def lane(shape):
    return lax.broadcasted_iota(jnp.int32, shape, 1)


def row(shape):
    return lax.broadcasted_iota(jnp.int32, shape, 0)


def in_pairs(ref, count):
    return [
        ref[2 * i] + pltpu.roll(ref[2 * i + 1], 64, 1) for i in range(count // 2)
    ]


def exchange(
    points,
    charges,
    leaf_skel,
    source_basis,
    leaf_upward,
    node_upward,
    points_low,
    points_high,
    charges_low,
    charges_high,
    skel_low,
    skel_high,
    leaf_low,
    leaf_high,
    leaf_charges,
    nodes_out,
    groups_out,
    basis,
    own_upward,
    nodes,
    groups,
    node_mine,
    group_mine,
    load_sem,
    halo_send,
    halo_recv,
    node_send,
    node_recv,
    group_send,
    group_recv,
):
    n_wide, n_narrow = lax.axis_size("wide"), lax.axis_size("narrow")
    g, n = lax.axis_index("wide"), lax.axis_index("narrow")
    at_end = (n == n_narrow - 1).astype(jnp.int32)
    at_start = (n == 0).astype(jnp.int32)
    after = (lax.rem(g + at_end, n_wide), lax.rem(n + 1, n_narrow))
    before = (
        lax.rem(g - at_start + n_wide, n_wide),
        lax.rem(n - 1 + n_narrow, n_narrow),
    )

    load_basis = pltpu.make_async_copy(source_basis, basis, load_sem.at[0])
    load_basis.start()
    load_upward = pltpu.make_async_copy(
        node_upward.at[:, pl.ds(pl.multiple_of(g * (64 * n_narrow), 128), 64 * n_narrow)],
        own_upward,
        load_sem.at[1],
    )
    load_upward.start()

    barrier = pltpu.get_barrier_semaphore()
    for device in (after, before):
        pl.semaphore_signal(barrier, inc=1, device_id=device, device_id_type=MESH)
    for step in range(1, n_narrow):
        pl.semaphore_signal(
            barrier, inc=1, device_id=(g, lax.rem(n + step, n_narrow)), device_id_type=MESH
        )
    for step in range(1, n_wide):
        pl.semaphore_signal(
            barrier, inc=1, device_id=(lax.rem(g + step, n_wide), n), device_id_type=MESH
        )
    pl.semaphore_wait(barrier, n_narrow + n_wide)

    def send(source, low, high, at):
        copies = []
        for target, device, k in ((low, after, 2 * at), (high, before, 2 * at + 1)):
            copy = pltpu.make_async_remote_copy(
                src_ref=source,
                dst_ref=target,
                send_sem=halo_send.at[k],
                recv_sem=halo_recv.at[k],
                device_id=device,
                device_id_type=MESH,
            )
            copy.start()
            copies.append(copy)
        return copies

    halo = send(points, points_low, points_high, 0)
    halo += send(charges, charges_low, charges_high, 1)
    halo += send(leaf_skel, skel_low, skel_high, 2)

    load_basis.wait()

    def upward(i, total):
        first = charges[:, pl.ds(pl.multiple_of(i * 256, 256), 128)]
        second = charges[:, pl.ds(pl.multiple_of(i * 256 + 128, 128), 128)]
        weights = jnp.concatenate([twice(first), twice(second)], axis=0)
        product = dot(weights, beside(basis[i]), NT)
        values = jnp.where(
            lane((16, 128)) < 64,
            product[0:16] + product[16:32],
            product[32:48] + product[48:64],
        )
        at = pl.ds(pl.multiple_of(i * 128, 128), 128)
        leaf_charges[:, at] = values
        return total + dot(twice(values), beside(leaf_upward[:, at]), NT)

    total = lax.fori_loop(
        0, basis.shape[0], upward, jnp.zeros((32, 64), F32), unroll=4
    )
    own = total[:16] + total[16:]
    own = jnp.concatenate([own, jnp.zeros_like(own)], axis=1)
    node_mine[...] = own
    halo += send(leaf_charges, leaf_low, leaf_high, 3)

    def gather(count, mine, table, device_of, place, send_sems, recv_sems):
        def one(step):
            return pltpu.make_async_remote_copy(
                src_ref=mine,
                dst_ref=table.at[place],
                send_sem=send_sems.at[step],
                recv_sem=recv_sems.at[step],
                device_id=device_of(step),
                device_id_type=MESH,
            )

        copies = [one(step) for step in range(1, count)]
        for copy in copies:
            copy.start()
        table[place] = mine[...]
        for copy in copies:
            copy.wait()

    gather(
        n_narrow, node_mine, nodes, lambda step: (g, lax.rem(n + step, n_narrow)), n, node_send, node_recv
    )
    load_upward.wait()
    group = jnp.zeros((16, 64), F32)
    for i, pair in enumerate(in_pairs(nodes, n_narrow)):
        group = group + dot(pair, own_upward[:, 128 * i : 128 * (i + 1)], NT, HIGH)
    group_mine[...] = jnp.concatenate([group, jnp.zeros_like(group)], axis=1)
    gather(
        n_wide, group_mine, groups, lambda step: (lax.rem(g + step, n_wide), n), g, group_send, group_recv
    )
    nodes_out[...] = nodes[...]
    groups_out[...] = groups[...]
    for copy in halo:
        copy.wait()


def source_tile(ref, start, width):
    return [
        jnp.broadcast_to(ref[k : k + 1, pl.ds(start, width)], (8, width)) for k in range(6)
    ]


def source_values(rows):
    y0, y1, y2, m0, m1, m2 = rows
    at = row(y0.shape)
    square = y0 * y0 + y1 * y1 + y2 * y2 + SMOOTH
    flux = (y0 * m0 + y1 * m1 + y2 * m2) * (-COEFFICIENT)
    one, zero = jnp.ones_like(y0), jnp.zeros_like(y0)

    def pick(*terms):
        out = zero
        for k in reversed(range(len(terms))):
            out = jnp.where(at == k, terms[k], out)
        return out

    return (
        pick(-2.0 * y0, -2.0 * y1, -2.0 * y2, square, one),
        pick(COEFFICIENT * m0, COEFFICIENT * m1, COEFFICIENT * m2, flux),
    )


def source_parts(values):
    first, second, third = pieces(values)
    return jnp.concatenate([first, second, third, first, second, first], axis=0).astype(BF16)


def target_parts(rows):
    x0, x1, x2 = rows[:3]
    at = row(x0.shape)
    square = x0 * x0 + x1 * x1 + x2 * x2
    values = jnp.where(at == 0, x0, jnp.where(at == 1, x1, jnp.where(at == 2, x2, 0.0)))
    values = jnp.where(at == 3, 1.0, jnp.where(at == 4, square, values))
    first, second, third = pieces(values)
    fill = jnp.zeros((80, values.shape[1]), F32)
    stacked = jnp.concatenate([first, first, first, second, second, third, fill], axis=0)
    return stacked.T.astype(BF16)[:, :48]


def block(targets, sources):
    both = dot(targets, sources, NN)
    width = both.shape[1] // 2
    root = lax.rsqrt(both[:, :width])
    return beside((both[:, width:] * root) * (root * root))


def pair_kernel(target, source):
    offset = [target[:, k : k + 1] - source[k : k + 1] for k in range(3)]
    distance = offset[0] * offset[0] + offset[1] * offset[1] + offset[2] * offset[2] + SMOOTH
    flux = offset[0] * source[3:4] + offset[1] * source[4:5] + offset[2] * source[5:6]
    root = lax.rsqrt(distance)
    return (flux * root) * (root * root) * COEFFICIENT


def couplings(
    near_pairs,
    leaf_links,
    node_links,
    group_links,
    points_low,
    points_own,
    points_high,
    charges_low,
    charges_own,
    charges_high,
    skel_low,
    skel_own,
    skel_high,
    leaf_low,
    leaf_own,
    leaf_high,
    node_skel,
    group_skel,
    node_downward,
    nodes,
    groups,
    near,
    couple,
    fields,
    near_sources,
    near_weights,
    near_targets,
    far_sources,
    far_weights,
    far_targets,
):
    n_narrow = lax.axis_size("narrow")
    g, n = lax.axis_index("wide"), lax.axis_index("narrow")
    leaves = leaf_links.shape[0]
    first_leaf = (g * n_narrow + n) * leaves - leaves
    spare = 3 * leaves

    def half_of(skel, start, which):
        tile = source_tile(skel, pl.multiple_of(start, 128), 128)
        at = row((8, 128))
        values = jnp.where(at == 0, tile[0], jnp.where(at == 1, tile[1], tile[2]))
        values = jnp.where(which == 0, values, pltpu.roll(values, 64, 1))
        return values.T[:64]

    def marked(links, base, count):
        at = lane((1, 64 * count)) // 64
        hit = at < 0
        for k in range(links.shape[1]):
            hit = hit | (at == links[0, k] - base)
        return hit.astype(F32)

    def small(target, skel, values, mark):
        out = jnp.zeros((16, 64), F32)
        for i, value in enumerate(values):
            span = slice(128 * i, 128 * (i + 1))
            kernel = pair_kernel(target, skel[:, span]) * mark[:, span]
            out = out + dot(value, kernel, NT, HIGH)
        return out

    group_count = groups.shape[0]
    group_fields = small(
        half_of(group_skel, (g // 2) * 128, lax.rem(g, 2)),
        group_skel[...],
        in_pairs(groups, group_count),
        marked(group_links, 0, group_count),
    )
    own_span = pl.ds(pl.multiple_of(g * (64 * n_narrow), 128), 64 * n_narrow)
    node_fields = dot(group_fields, node_downward[...], NN, HIGH) + small(
        half_of(node_skel, g * (64 * n_narrow) + (n // 2) * 128, lax.rem(n, 2)),
        node_skel[:, own_span],
        in_pairs(nodes, n_narrow),
        marked(node_links, g * n_narrow, n_narrow),
    )
    fields[...] = node_fields

    near[...] = jnp.zeros_like(near)
    zero_rows = [jnp.zeros((8, 128), F32)] * 6
    for table in (near_sources, far_sources):
        parts = [source_parts(v) for v in source_values(zero_rows)]
        table[spare] = jnp.concatenate(parts, axis=1)
    for table in (near_weights, far_weights):
        table[spare] = jnp.zeros(table.shape[1:], BF16)

    for side, (points, charges) in enumerate(
        ((points_low, charges_low), (points_own, charges_own), (points_high, charges_high))
    ):

        def near_prepare(i, carry, side=side, points=points, charges=charges):
            start = pl.multiple_of(i * 128, 128)
            rows = source_tile(points, start, 128)
            parts = [source_parts(v) for v in source_values(rows)]
            near_sources[side * leaves + i] = jnp.concatenate(parts, axis=1)
            near_weights[side * leaves + i] = twice(charges[:, pl.ds(start, 128)])
            if side == 1:
                near_targets[i] = target_parts(rows)
            return carry

        lax.fori_loop(0, leaves, near_prepare, 0, unroll=4)

    def near_step(i, carry):
        parts = []
        for k in range(NEAR_STEP):
            code = near_pairs[0, i * NEAR_STEP + k]
            t, s = code // 1024, lax.rem(code, 1024)
            w = jnp.where(s >= 256, spare, s)
            s = jnp.where(s >= 256, spare, s)
            sums = dot(near_weights[w], block(near_targets[t], near_sources[s]), NT)
            parts.append((t, sums[:16] + sums[16:]))
        for t, part in parts:
            at = pl.ds(pl.multiple_of(t * 128, 128), 128)
            near[:, at] = near[:, at] + part
        return carry

    lax.fori_loop(0, NEAR_PAIRS // NEAR_STEP, near_step, 0)

    def both_halves(x):
        low = lane(x.shape) < 64
        turned = pltpu.roll(x, 64, 1)
        return jnp.where(low, x, turned), jnp.where(low, turned, x)

    for side, (points, charges) in enumerate(
        ((skel_low, leaf_low), (skel_own, leaf_own), (skel_high, leaf_high))
    ):

        def far_prepare(i, carry, side=side, points=points, charges=charges):
            start = pl.multiple_of(i * 128, 128)
            rows = source_tile(points, start, 128)
            split = [both_halves(v) for v in source_values(rows)]
            weights = both_halves(charges[:, pl.ds(start, 128)])
            for k in range(2):
                parts = [source_parts(v[k]) for v in split]
                far_sources[side * leaves + 2 * i + k] = jnp.concatenate(parts, axis=1)
                far_weights[side * leaves + 2 * i + k] = twice(weights[k])
            if side == 1:
                targets = target_parts(rows)
                far_targets[2 * i] = targets[:64]
                far_targets[2 * i + 1] = targets[64:]
            return carry

        lax.fori_loop(0, leaves // 2, far_prepare, 0, unroll=2)

    low_s = (lax.rem(lane((48, 256)), 128) < 64).astype(F32).astype(BF16)
    high_s = jnp.ones_like(low_s) - low_s
    low_w, high_w = low_s[:32], high_s[:32]

    def local(leaf, slot):
        entry = leaf_links[leaf, slot]
        return jnp.where(entry < 0, spare, entry - first_leaf)

    def far_step(i, carry):
        sums = []
        for k in range(2):
            leaf = 2 * i + k
            out = jnp.zeros((32, 64), F32)
            for slot in range(0, leaf_links.shape[1], 2):
                a, b = local(leaf, slot), local(leaf, slot + 1)
                sources = far_sources[a] * low_s + far_sources[b] * high_s
                weights = far_weights[a] * low_w + far_weights[b] * high_w
                out = out + dot(weights, block(far_targets[leaf], sources), NT)
            sums.append(out[:16] + out[16:])
        couple[:, pl.ds(pl.multiple_of(i * 128, 128), 128)] = jnp.concatenate(sums, axis=1)
        return carry

    lax.fori_loop(0, leaves // 2, far_step, 0)


def compact(near_list, first_leaf, leaves):
    flat = near_list.reshape(-1)
    count = flat.shape[0]
    used = flat >= 0
    ids = jnp.arange(count, dtype=jnp.int32)
    code = (ids // near_list.shape[1]) * 1024 + flat - first_leaf
    earlier = (ids[None, :] < ids[:, None]) & used[None, :]
    place = jnp.where(used, jnp.sum(earlier.astype(jnp.int32), axis=1), -1)
    slots = jnp.arange(NEAR_PAIRS, dtype=jnp.int32)
    hit = place[None, :] == slots[:, None]
    packed = jnp.sum(jnp.where(hit, code[None, :], 0), axis=1)
    total = jnp.sum(used.astype(jnp.int32))
    return jnp.where(slots < total, packed, 256)[None, :]


def on_device(
    points,
    charges,
    leaf_skel,
    node_skel,
    group_skel,
    source_basis,
    target_basis,
    leaf_upward,
    leaf_downward,
    node_upward,
    node_downward,
    near_list,
    leaf_links,
    node_links,
    group_links,
):
    n_wide, n_narrow = lax.axis_size("wide"), lax.axis_size("narrow")
    leaves, rank = source_basis.shape[0], source_basis.shape[1]
    first_leaf = (lax.axis_index("wide") * n_narrow + lax.axis_index("narrow")) * leaves - leaves
    vmem = pl.BlockSpec(memory_space=pltpu.VMEM)
    smem = pl.BlockSpec(memory_space=pltpu.SMEM)
    anywhere = pl.BlockSpec(memory_space=pl.ANY)

    def like(x):
        return jax.ShapeDtypeStruct(x.shape, F32)

    leaf_shape = jax.ShapeDtypeStruct((16, leaf_skel.shape[1]), F32)
    table = (16, 128)
    out = pl.pallas_call(
        exchange,
        out_shape=[
            like(points),
            like(points),
            like(charges),
            like(charges),
            like(leaf_skel),
            like(leaf_skel),
            leaf_shape,
            leaf_shape,
            leaf_shape,
            jax.ShapeDtypeStruct((n_narrow, *table), F32),
            jax.ShapeDtypeStruct((n_wide, *table), F32),
        ],
        in_specs=[anywhere, vmem, anywhere, anywhere, vmem, anywhere],
        out_specs=[anywhere] * 8 + [vmem] * 3,
        scratch_shapes=[
            pltpu.VMEM((leaves // 2, 2 * rank, source_basis.shape[2]), F32),
            pltpu.VMEM((64, 64 * n_narrow), F32),
            pltpu.VMEM((n_narrow, *table), F32),
            pltpu.VMEM((n_wide, *table), F32),
            pltpu.VMEM(table, F32),
            pltpu.VMEM(table, F32),
            pltpu.SemaphoreType.DMA((2,)),
            pltpu.SemaphoreType.DMA((8,)),
            pltpu.SemaphoreType.DMA((8,)),
            pltpu.SemaphoreType.DMA((n_narrow,)),
            pltpu.SemaphoreType.DMA((n_narrow,)),
            pltpu.SemaphoreType.DMA((n_wide,)),
            pltpu.SemaphoreType.DMA((n_wide,)),
        ],
        compiler_params=pltpu.CompilerParams(
            collective_id=0, has_side_effects=True, vmem_limit_bytes=VMEM_LIMIT
        ),
        name="exchange",
    )(
        points,
        charges,
        leaf_skel,
        source_basis.reshape(leaves // 2, 2 * rank, source_basis.shape[2]),
        leaf_upward,
        node_upward,
    )
    p_low, p_high, c_low, c_high, s_low, s_high, l_low, l_high, l_own, nodes, groups = out

    tables = 3 * leaves + 1
    near, couple, fields = pl.pallas_call(
        couplings,
        out_shape=[
            like(charges),
            leaf_shape,
            jax.ShapeDtypeStruct((16, rank), F32),
        ],
        in_specs=[smem] * 4 + [vmem] * 17,
        out_specs=[vmem] * 3,
        scratch_shapes=[
            pltpu.VMEM((tables, 48, 256), BF16),
            pltpu.VMEM((tables, 32, 256), BF16),
            pltpu.VMEM((leaves, 128, 48), BF16),
            pltpu.VMEM((tables, 48, 256), BF16),
            pltpu.VMEM((tables, 32, 256), BF16),
            pltpu.VMEM((leaves, 64, 48), BF16),
        ],
        compiler_params=pltpu.CompilerParams(vmem_limit_bytes=VMEM_LIMIT),
        name="couplings",
    )(
        compact(near_list, first_leaf, leaves),
        leaf_links,
        node_links,
        group_links,
        p_low,
        points,
        p_high,
        c_low,
        charges,
        c_high,
        s_low,
        leaf_skel,
        s_high,
        l_low,
        l_own,
        l_high,
        node_skel,
        group_skel,
        node_downward,
        nodes,
        groups,
    )
    leaf_fields = (jnp.dot(fields, leaf_downward, precision=HIGH) + couple).reshape(16, leaves, rank)
    far = jnp.einsum("qlr,lrp->qlp", leaf_fields, target_basis, precision=HIGH)
    return near + far.reshape(near.shape)


def solution(mesh):
    both = ("wide", "narrow")
    in_specs = (
        P(None, both),
        P(None, both),
        P(None, both),
        P(),
        P(),
        P(both, None, None),
        P(both, None, None),
        P(None, both),
        P(None, both),
        P(),
        P(None, both),
        P(both, None),
        P(both, None),
        P(both, None),
        P("wide", None),
    )
    return jax.shard_map(
        on_device, mesh=mesh, in_specs=in_specs, out_specs=P(None, both), check_vma=False
    )
```

```python
import math

import jax
import jax.numpy as jnp
from jax import lax
from jax.experimental import pallas as pl
from jax.experimental.pallas import tpu as pltpu
from jax.sharding import PartitionSpec as P

MESH = pl.DeviceIdType.MESH
HIGH = lax.Precision.HIGHEST
F32, BF16 = jnp.float32, jnp.bfloat16
SMOOTH = 0.25
COEFFICIENT = 1.0 / (4.0 * math.pi)
NT = (((1,), (1,)), ((), ()))
NN = (((1,), (0,)), ((), ()))
NEAR_REST = 288 - 64
NEAR_STEP = 32
FAR_STEP = 8
VMEM_LIMIT = 56 * 2**20


def dot(a, b, dims, precision=None):
    return lax.dot_general(a, b, dims, precision=precision, preferred_element_type=F32)


def halves(x):
    high = x.astype(BF16)
    return high, (x - high.astype(F32)).astype(BF16)


def twice(x):
    high, low = halves(x)
    stacked = jnp.concatenate([high, low], axis=0)
    return jnp.concatenate([stacked, stacked], axis=1)


def beside(x):
    high, low = halves(x)
    return jnp.concatenate([high, low], axis=1)


def pieces(x):
    first = x.astype(BF16).astype(F32)
    rest = x - first
    second = rest.astype(BF16).astype(F32)
    return first, second, rest - second


def lane(shape):
    return lax.broadcasted_iota(jnp.int32, shape, 1)


def row(shape):
    return lax.broadcasted_iota(jnp.int32, shape, 0)


def in_pairs(ref, count):
    return [
        ref[2 * i] + pltpu.roll(ref[2 * i + 1], 64, 1) for i in range(count // 2)
    ]


def source_tile(ref, start, width):
    return [
        jnp.broadcast_to(ref[k : k + 1, pl.ds(start, width)], (8, width)) for k in range(6)
    ]


def source_values(rows):
    y0, y1, y2, m0, m1, m2 = rows
    at = row(y0.shape)
    square = y0 * y0 + y1 * y1 + y2 * y2 + SMOOTH
    flux = (y0 * m0 + y1 * m1 + y2 * m2) * (-COEFFICIENT)
    one, zero = jnp.ones_like(y0), jnp.zeros_like(y0)

    def pick(*terms):
        out = zero
        for k in reversed(range(len(terms))):
            out = jnp.where(at == k, terms[k], out)
        return out

    return (
        pick(-2.0 * y0, -2.0 * y1, -2.0 * y2, square, one),
        pick(COEFFICIENT * m0, COEFFICIENT * m1, COEFFICIENT * m2, flux),
    )


def source_parts(values):
    first, second, third = pieces(values)
    return jnp.concatenate([first, second, third, first, second, first], axis=0).astype(BF16)


def target_parts(rows):
    x0, x1, x2 = rows[:3]
    at = row(x0.shape)
    square = x0 * x0 + x1 * x1 + x2 * x2
    values = jnp.where(at == 0, x0, jnp.where(at == 1, x1, jnp.where(at == 2, x2, 0.0)))
    values = jnp.where(at == 3, 1.0, jnp.where(at == 4, square, values))
    first, second, third = pieces(values)
    fill = jnp.zeros((80, values.shape[1]), F32)
    stacked = jnp.concatenate([first, first, first, second, second, third, fill], axis=0)
    return stacked.T.astype(BF16)[:, :48]


def kernel_block(targets, sources):
    both = dot(targets, sources, NN)
    width = both.shape[1] // 2
    root = lax.rsqrt(both[:, :width])
    return beside((both[:, width:] * root) * (root * root))


def pair_kernel(target, source):
    offset = [target[:, k : k + 1] - source[k : k + 1] for k in range(3)]
    distance = offset[0] * offset[0] + offset[1] * offset[1] + offset[2] * offset[2] + SMOOTH
    flux = offset[0] * source[3:4] + offset[1] * source[4:5] + offset[2] * source[5:6]
    root = lax.rsqrt(distance)
    return (flux * root) * (root * root) * COEFFICIENT


def fused(
    near_codes,
    near_places,
    far_codes,
    node_links,
    group_links,
    points,
    charges,
    leaf_skel,
    source_basis,
    leaf_upward,
    node_upward,
    node_skel,
    target_basis,
    leaf_downward,
    node_downward,
    group_skel,
    out,
    p_low,
    p_own,
    p_high,
    c_low,
    c_own,
    c_high,
    s_low,
    s_own,
    s_high,
    l_low,
    l_own,
    l_high,
    basis_up,
    basis_down,
    upward_own,
    downward_own,
    group_upward,
    nodes_skel,
    nodes,
    groups,
    node_mine,
    group_mine,
    near_sources,
    near_weights,
    near_targets,
    near_blocks,
    near_parts,
    far_sources,
    far_weights,
    far_targets,
    far_blocks,
    couple,
    load_sem,
    halo_send,
    halo_recv,
    node_send,
    node_recv,
    group_send,
    group_recv,
):
    n_wide, n_narrow = lax.axis_size("wide"), lax.axis_size("narrow")
    g, n = lax.axis_index("wide"), lax.axis_index("narrow")
    leaves = far_codes.shape[1]
    spare = 3 * leaves
    at_end = (n == n_narrow - 1).astype(jnp.int32)
    at_start = (n == 0).astype(jnp.int32)
    after = (lax.rem(g + at_end, n_wide), lax.rem(n + 1, n_narrow))
    before = (
        lax.rem(g - at_start + n_wide, n_wide),
        lax.rem(n - 1 + n_narrow, n_narrow),
    )
    group_span = pl.ds(pl.multiple_of(g * (64 * n_narrow), 128), 64 * n_narrow)

    loads = []
    for k, (source, target) in enumerate(
        (
            (charges, c_own),
            (source_basis, basis_up),
            (leaf_upward, upward_own),
            (points, p_own),
            (leaf_skel, s_own),
            (node_upward.at[:, group_span], group_upward),
            (node_skel.at[:, group_span], nodes_skel),
            (leaf_downward, downward_own),
            (target_basis, basis_down),
        )
    ):
        copy = pltpu.make_async_copy(source, target, load_sem.at[k])
        copy.start()
        loads.append(copy)

    barrier = pltpu.get_barrier_semaphore()
    for device in (after, before):
        pl.semaphore_signal(barrier, inc=1, device_id=device, device_id_type=MESH)
    for step in range(1, n_narrow):
        pl.semaphore_signal(
            barrier, inc=1, device_id=(g, lax.rem(n + step, n_narrow)), device_id_type=MESH
        )
    for step in range(1, n_wide):
        pl.semaphore_signal(
            barrier, inc=1, device_id=(lax.rem(g + step, n_wide), n), device_id_type=MESH
        )
    pl.semaphore_wait(barrier, n_narrow + n_wide)

    def send(source, low, high, at):
        copies = []
        for target, device, k in ((low, after, 2 * at), (high, before, 2 * at + 1)):
            copy = pltpu.make_async_remote_copy(
                src_ref=source,
                dst_ref=target,
                send_sem=halo_send.at[k],
                recv_sem=halo_recv.at[k],
                device_id=device,
                device_id_type=MESH,
            )
            copy.start()
            copies.append(copy)
        return copies

    near_halo = send(points, p_low, p_high, 0) + send(charges, c_low, c_high, 1)

    for copy in loads[:3]:
        copy.wait()

    def upward(i, total):
        first = c_own[:, pl.ds(pl.multiple_of(i * 256, 256), 128)]
        second = c_own[:, pl.ds(pl.multiple_of(i * 256 + 128, 128), 128)]
        weights = jnp.concatenate([twice(first), twice(second)], axis=0)
        product = dot(weights, beside(basis_up[i]), NT)
        values = jnp.where(
            lane((16, 128)) < 64,
            product[0:16] + product[16:32],
            product[32:48] + product[48:64],
        )
        at = pl.ds(pl.multiple_of(i * 128, 128), 128)
        l_own[:, at] = values
        return total + dot(twice(values), beside(upward_own[:, at]), NT)

    total = lax.fori_loop(0, leaves // 2, upward, jnp.zeros((32, 64), F32), unroll=8)
    own = total[:16] + total[16:]
    node_mine[...] = jnp.concatenate([own, jnp.zeros_like(own)], axis=1)

    def gather(count, mine, table, device_of, place, send_sems, recv_sems):
        copies = []
        for step in range(1, count):
            copy = pltpu.make_async_remote_copy(
                src_ref=mine,
                dst_ref=table.at[place],
                send_sem=send_sems.at[step],
                recv_sem=recv_sems.at[step],
                device_id=device_of(step),
                device_id_type=MESH,
            )
            copy.start()
            copies.append(copy)
        table[place] = mine[...]
        return copies

    node_copies = gather(
        n_narrow, node_mine, nodes, lambda step: (g, lax.rem(n + step, n_narrow)), n, node_send, node_recv
    )
    far_halo = send(leaf_skel, s_low, s_high, 2) + send(l_own, l_low, l_high, 3)

    zero_rows = [jnp.zeros((8, 128), F32)] * 6
    for table in (near_sources, far_sources):
        parts = [source_parts(v) for v in source_values(zero_rows)]
        table[spare] = jnp.concatenate(parts, axis=1)
    for table in (near_weights, far_weights):
        table[spare] = jnp.zeros(table.shape[1:], BF16)

    def prepare_near(side, points_ref, charges_ref):
        def body(i, carry):
            start = pl.multiple_of(i * 128, 128)
            rows = source_tile(points_ref, start, 128)
            parts = [source_parts(v) for v in source_values(rows)]
            near_sources[side * leaves + i] = jnp.concatenate(parts, axis=1)
            near_weights[side * leaves + i] = twice(charges_ref[:, pl.ds(start, 128)])
            if side == 1:
                near_targets[i] = target_parts(rows)
            return carry

        lax.fori_loop(0, leaves, body, 0, unroll=4)

    def both_halves(x):
        low = lane(x.shape) < 64
        turned = pltpu.roll(x, 64, 1)
        return jnp.where(low, x, turned), jnp.where(low, turned, x)

    def prepare_far(side, points_ref, charges_ref):
        def body(i, carry):
            start = pl.multiple_of(i * 128, 128)
            rows = source_tile(points_ref, start, 128)
            split = [both_halves(v) for v in source_values(rows)]
            weights = both_halves(charges_ref[:, pl.ds(start, 128)])
            for k in range(2):
                parts = [source_parts(v[k]) for v in split]
                far_sources[side * leaves + 2 * i + k] = jnp.concatenate(parts, axis=1)
                far_weights[side * leaves + 2 * i + k] = twice(weights[k])
            if side == 1:
                targets = target_parts(rows)
                far_targets[2 * i] = targets[:64]
                far_targets[2 * i + 1] = targets[64:]
            return carry

        lax.fori_loop(0, leaves // 2, body, 0, unroll=4)

    def stream(count, first, second):
        first(0)

        def body(i, carry):
            second(i - 1)
            first(i)
            return carry

        lax.fori_loop(1, count, body, 0)
        second(count - 1)

    loads[3].wait()
    prepare_near(1, p_own, c_own)

    def self_first(i):
        for k in range(NEAR_STEP):
            leaf = i * NEAR_STEP + k
            near_blocks[k] = kernel_block(near_targets[leaf], near_sources[leaves + leaf])

    def self_second(i):
        for k in range(NEAR_STEP):
            leaf = i * NEAR_STEP + k
            sums = dot(near_weights[leaves + leaf], near_blocks[k], NT)
            out[:, pl.ds(pl.multiple_of(leaf * 128, 128), 128)] = sums[:16] + sums[16:]

    stream(leaves // NEAR_STEP, self_first, self_second)

    loads[4].wait()
    prepare_far(1, s_own, l_own)

    for copy in node_copies:
        copy.wait()
    loads[5].wait()
    group = jnp.zeros((16, 64), F32)
    for i, pair in enumerate(in_pairs(nodes, n_narrow)):
        group = group + dot(pair, group_upward[:, 128 * i : 128 * (i + 1)], NT, HIGH)
    group_mine[...] = jnp.concatenate([group, jnp.zeros_like(group)], axis=1)
    group_copies = gather(
        n_wide, group_mine, groups, lambda step: (lax.rem(g + step, n_wide), n), g, group_send, group_recv
    )

    for copy in near_halo:
        copy.wait()
    prepare_near(0, p_low, c_low)
    prepare_near(2, p_high, c_high)

    def near_code(i, k):
        code = near_codes[0, i * NEAR_STEP + k]
        return code // 1024, lax.rem(code, 1024)

    def near_first(i):
        for k in range(NEAR_STEP):
            t, s = near_code(i, k)
            near_blocks[k] = kernel_block(near_targets[t], near_sources[s])

    def near_second(i):
        for k in range(NEAR_STEP):
            _, s = near_code(i, k)
            sums = dot(near_weights[s], near_blocks[k], NT)
            near_parts[i * NEAR_STEP + k] = sums[:16] + sums[16:]

    stream(NEAR_REST // NEAR_STEP, near_first, near_second)
    near_parts[NEAR_REST] = jnp.zeros((16, 128), F32)

    for copy in far_halo:
        copy.wait()
    prepare_far(0, s_low, l_low)
    prepare_far(2, s_high, l_high)

    low_s = (lax.rem(lane((48, 256)), 128) < 64).astype(F32).astype(BF16)
    high_s = jnp.ones_like(low_s) - low_s
    low_w, high_w = low_s[:32], high_s[:32]
    far_slots = far_codes.shape[0]

    def far_picks(i):
        for k in range(FAR_STEP):
            for slot in range(0, far_slots, 2):
                leaf = FAR_STEP * i + k
                yield k, slot // 2, leaf, far_codes[slot, leaf], far_codes[slot + 1, leaf]

    def far_first(i):
        for k, j, leaf, a, b in far_picks(i):
            sources = far_sources[a] * low_s + far_sources[b] * high_s
            far_blocks[k * (far_slots // 2) + j] = kernel_block(far_targets[leaf], sources)

    def far_second(i):
        sums = [jnp.zeros((32, 64), F32)] * FAR_STEP
        for k, j, _, a, b in far_picks(i):
            weights = far_weights[a] * low_w + far_weights[b] * high_w
            sums[k] = sums[k] + dot(weights, far_blocks[k * (far_slots // 2) + j], NT)
        sums = [x[:16] + x[16:] for x in sums]
        for k in range(0, FAR_STEP, 2):
            at = pl.ds(pl.multiple_of((FAR_STEP * i + k) * 64, 128), 128)
            couple[:, at] = jnp.concatenate(sums[k : k + 2], axis=1)

    stream(leaves // FAR_STEP, far_first, far_second)

    for copy in group_copies:
        copy.wait()
    loads[6].wait()

    def half_of(skel, start, which):
        tile = source_tile(skel, pl.multiple_of(start, 128), 128)
        at = row((8, 128))
        values = jnp.where(at == 0, tile[0], jnp.where(at == 1, tile[1], tile[2]))
        values = jnp.where(which == 0, values, pltpu.roll(values, 64, 1))
        return values.T[:64]

    def marked(links, base, count):
        at = lane((1, 64 * count)) // 64
        hit = at < 0
        for k in range(links.shape[1]):
            hit = hit | (at == links[0, k] - base)
        return hit.astype(F32)

    def small(target, skel, values, mark):
        sums = jnp.zeros((16, 64), F32)
        for i, value in enumerate(values):
            span = slice(128 * i, 128 * (i + 1))
            kernel = pair_kernel(target, skel[:, span]) * mark[:, span]
            sums = sums + dot(value, kernel, NT, HIGH)
        return sums

    group_fields = small(
        half_of(group_skel, (g // 2) * 128, lax.rem(g, 2)),
        group_skel[...],
        in_pairs(groups, n_wide),
        marked(group_links, 0, n_wide),
    )
    node_fields = dot(group_fields, node_downward[...], NN, HIGH) + small(
        half_of(nodes_skel, (n // 2) * 128, lax.rem(n, 2)),
        nodes_skel[...],
        in_pairs(nodes, n_narrow),
        marked(node_links, g * n_narrow, n_narrow),
    )
    field_halves = jnp.concatenate(halves(node_fields), axis=0)

    loads[7].wait()
    loads[8].wait()

    def downward(i, carry):
        at = pl.ds(pl.multiple_of(i * 128, 128), 128)
        product = dot(field_halves, beside(downward_own[:, at]), NN)
        fields = product[:16, :128] + product[16:, :128] + product[:16, 128:] + couple[:, at]
        low = lane((16, 128)) < 64
        lefts = [jnp.where(low, fields, 0.0), jnp.where(low, 0.0, fields)]
        left = jnp.concatenate([h for x in lefts for h in halves(x)], axis=0)
        product = dot(left, beside(basis_down[i]), NN)
        for k in range(2):
            leaf = 2 * i + k
            rows = product[32 * k : 32 * (k + 1)]
            value = rows[:16, :128] + rows[16:, :128] + rows[:16, 128:]
            for slot in range(near_places.shape[0]):
                value = value + near_parts[near_places[slot, leaf]]
            span = pl.ds(pl.multiple_of(leaf * 128, 128), 128)
            out[:, span] = out[:, span] + value
        return carry

    lax.fori_loop(0, leaves // 2, downward, 0, unroll=4)


def compact(near_list, first_leaf, leaves):
    rest = near_list.T[1:]
    flat = rest.reshape(-1)
    used = flat >= 0
    ids = jnp.arange(flat.shape[0], dtype=jnp.int32)
    code = lax.rem(ids, leaves) * 1024 + flat - first_leaf
    earlier = (ids[None, :] < ids[:, None]) & used[None, :]
    place = jnp.where(used, jnp.sum(earlier.astype(jnp.int32), axis=1), NEAR_REST)
    slots = jnp.arange(NEAR_REST, dtype=jnp.int32)
    hit = place[None, :] == slots[:, None]
    packed = jnp.sum(jnp.where(hit, code[None, :] + 1, 0), axis=1)
    codes = jnp.where(packed > 0, packed - 1, 3 * leaves)
    return codes[None, :], place.reshape(rest.shape)


def on_device(
    points,
    charges,
    leaf_skel,
    node_skel,
    group_skel,
    source_basis,
    target_basis,
    leaf_upward,
    leaf_downward,
    node_upward,
    node_downward,
    near_list,
    leaf_links,
    node_links,
    group_links,
):
    n_wide, n_narrow = lax.axis_size("wide"), lax.axis_size("narrow")
    leaves, rank, size = source_basis.shape
    first_leaf = (lax.axis_index("wide") * n_narrow + lax.axis_index("narrow")) * leaves - leaves
    vmem = pl.BlockSpec(memory_space=pltpu.VMEM)
    smem = pl.BlockSpec(memory_space=pltpu.SMEM)
    anywhere = pl.BlockSpec(memory_space=pl.ANY)
    tables = 3 * leaves + 1
    table = (16, 128)
    paired = (leaves // 2, 2 * rank, size)
    codes, places = compact(near_list, first_leaf, leaves)

    def f32(*shape):
        return pltpu.VMEM(shape, F32)

    def bf16(*shape):
        return pltpu.VMEM(shape, BF16)

    def sems(count):
        return pltpu.SemaphoreType.DMA((count,))

    return pl.pallas_call(
        fused,
        out_shape=jax.ShapeDtypeStruct(charges.shape, F32),
        in_specs=[smem] * 5 + [anywhere] * 9 + [vmem] * 2,
        out_specs=vmem,
        scratch_shapes=[
            *[f32(*points.shape)] * 3,
            *[f32(*charges.shape)] * 3,
            *[f32(*leaf_skel.shape)] * 3,
            *[f32(16, leaf_skel.shape[1])] * 3,
            f32(*paired),
            f32(*paired),
            f32(*leaf_upward.shape),
            f32(*leaf_downward.shape),
            f32(64, 64 * n_narrow),
            f32(6, 64 * n_narrow),
            f32(n_narrow, *table),
            f32(n_wide, *table),
            f32(*table),
            f32(*table),
            bf16(tables, 48, 256),
            bf16(tables, 32, 256),
            bf16(leaves, 128, 48),
            bf16(NEAR_STEP, 128, 256),
            f32(NEAR_REST + 1, *table),
            bf16(tables, 48, 256),
            bf16(tables, 32, 256),
            bf16(leaves, 64, 48),
            bf16(4 * FAR_STEP, 64, 256),
            f32(16, leaf_skel.shape[1]),
            sems(9),
            sems(8),
            sems(8),
            sems(n_narrow),
            sems(n_narrow),
            sems(n_wide),
            sems(n_wide),
        ],
        compiler_params=pltpu.CompilerParams(
            collective_id=0, has_side_effects=True, vmem_limit_bytes=VMEM_LIMIT
        ),
        name="fused",
    )(
        codes,
        places,
        jnp.where(leaf_links < 0, 3 * leaves, leaf_links - first_leaf).T,
        node_links,
        group_links,
        points,
        charges,
        leaf_skel,
        source_basis.reshape(paired),
        leaf_upward,
        node_upward,
        node_skel,
        target_basis.reshape(paired),
        leaf_downward,
        node_downward,
        group_skel,
    )


def solution(mesh):
    both = ("wide", "narrow")
    in_specs = (
        P(None, both),
        P(None, both),
        P(None, both),
        P(),
        P(),
        P(both, None, None),
        P(both, None, None),
        P(None, both),
        P(None, both),
        P(),
        P(None, both),
        P(both, None),
        P(both, None),
        P(both, None),
        P("wide", None),
    )
    return jax.shard_map(
        on_device, mesh=mesh, in_specs=in_specs, out_specs=P(None, both), check_vma=False
    )
```

```python
import math

import jax
import jax.numpy as jnp
from jax import lax
from jax.experimental import pallas as pl
from jax.experimental.pallas import tpu as pltpu
from jax.sharding import PartitionSpec as P

MESH = pl.DeviceIdType.MESH
HIGH = lax.Precision.HIGHEST
F32, BF16 = jnp.float32, jnp.bfloat16
SMOOTH = 0.25
COEFFICIENT = 1.0 / (4.0 * math.pi)
NT = (((1,), (1,)), ((), ()))
NN = (((1,), (0,)), ((), ()))
NEAR_REST = 288 - 64
NEAR_STEP = 32
FAR_STEP = 8
VMEM_LIMIT = 56 * 2**20


def dot(a, b, dims, precision=None):
    return lax.dot_general(a, b, dims, precision=precision, preferred_element_type=F32)


def halves(x):
    high = x.astype(BF16)
    return high, (x - high.astype(F32)).astype(BF16)


def twice(x):
    high, low = halves(x)
    stacked = jnp.concatenate([high, low], axis=0)
    return jnp.concatenate([stacked, stacked], axis=1)


def beside(x):
    high, low = halves(x)
    return jnp.concatenate([high, low], axis=1)


def pieces(x):
    first = x.astype(BF16).astype(F32)
    rest = x - first
    second = rest.astype(BF16).astype(F32)
    return first, second, rest - second


def lane(shape):
    return lax.broadcasted_iota(jnp.int32, shape, 1)


def row(shape):
    return lax.broadcasted_iota(jnp.int32, shape, 0)


def in_pairs(ref, count):
    return [
        ref[2 * i] + pltpu.roll(ref[2 * i + 1], 64, 1) for i in range(count // 2)
    ]


def source_tile(ref, start, width):
    return [
        jnp.broadcast_to(ref[k : k + 1, pl.ds(start, width)], (8, width)) for k in range(6)
    ]


def source_values(rows):
    y0, y1, y2, m0, m1, m2 = rows
    at = row(y0.shape)
    square = y0 * y0 + y1 * y1 + y2 * y2 + SMOOTH
    flux = (y0 * m0 + y1 * m1 + y2 * m2) * (-COEFFICIENT)
    one, zero = jnp.ones_like(y0), jnp.zeros_like(y0)

    def pick(*terms):
        out = zero
        for k in reversed(range(len(terms))):
            out = jnp.where(at == k, terms[k], out)
        return out

    return (
        pick(-2.0 * y0, -2.0 * y1, -2.0 * y2, square, one),
        pick(COEFFICIENT * m0, COEFFICIENT * m1, COEFFICIENT * m2, flux),
    )


def source_parts(values):
    first, second, third = pieces(values)
    return jnp.concatenate([first, second, third, first, second, first], axis=0).astype(BF16)


def target_parts(rows):
    x0, x1, x2 = rows[:3]
    at = row(x0.shape)
    square = x0 * x0 + x1 * x1 + x2 * x2
    values = jnp.where(at == 0, x0, jnp.where(at == 1, x1, jnp.where(at == 2, x2, 0.0)))
    values = jnp.where(at == 3, 1.0, jnp.where(at == 4, square, values))
    first, second, third = pieces(values)
    fill = jnp.zeros((80, values.shape[1]), F32)
    stacked = jnp.concatenate([first, first, first, second, second, third, fill], axis=0)
    return stacked.T.astype(BF16)[:, :48]


def kernel_block(targets, sources):
    both = dot(targets, sources, NN)
    width = both.shape[1] // 2
    root = lax.rsqrt(both[:, :width])
    return beside((both[:, width:] * root) * (root * root))


def pair_kernel(target, source):
    offset = [target[:, k : k + 1] - source[k : k + 1] for k in range(3)]
    distance = offset[0] * offset[0] + offset[1] * offset[1] + offset[2] * offset[2] + SMOOTH
    flux = offset[0] * source[3:4] + offset[1] * source[4:5] + offset[2] * source[5:6]
    root = lax.rsqrt(distance)
    return (flux * root) * (root * root) * COEFFICIENT


def lists(near, links, first_leaf):
    slots, leaves = near.shape
    fill = jnp.full((slots, 128 - leaves), -1, jnp.int32)
    near = jnp.concatenate([near, fill], axis=1)
    links = jnp.concatenate([links, fill], axis=1)
    spare = 3 * leaves
    far = jnp.where(links < 0, spare, jnp.clip(links - first_leaf, 0, spare - 1))
    across, down = lane(near.shape), row(near.shape)
    used = (near >= 0) & (down > 0)
    count = used.astype(jnp.int32)
    along = count
    step = 1
    while step < leaves:
        along = along + jnp.where(across >= step, pltpu.roll(along, step, 1), 0)
        step *= 2
    totals = jnp.broadcast_to(along[:, leaves - 1 : leaves], along.shape)
    above = totals
    step = 1
    while step < slots:
        above = above + jnp.where(down >= step, pltpu.roll(above, step, 0), 0)
        step *= 2
    place = along - count + above - totals
    place = jnp.where(used, jnp.minimum(place, NEAR_REST), NEAR_REST)
    code = across * 1024 + jnp.clip(near - first_leaf, 0, spare - 1) + 1
    places, codes = place.T[:leaves], code.T[:leaves]
    at = lane((leaves, 256))
    hits = jnp.zeros((leaves, 256), jnp.int32)
    for slot in range(1, slots):
        hits = hits + jnp.where(places[:, slot : slot + 1] == at, codes[:, slot : slot + 1], 0)
    packed = jnp.sum(hits, axis=0, keepdims=True)
    return jnp.where((packed > 0) & (lane((1, 256)) < NEAR_REST), packed - 1, spare), place, far


def fused(
    near_list,
    leaf_links,
    node_links,
    group_links,
    points,
    charges,
    leaf_skel,
    source_basis,
    leaf_upward,
    node_upward,
    node_skel,
    target_basis,
    leaf_downward,
    node_downward,
    group_skel,
    near_out,
    far_out,
    p_low,
    p_own,
    p_high,
    c_low,
    c_own,
    c_high,
    s_low,
    s_own,
    s_high,
    l_low,
    l_own,
    l_high,
    basis_up,
    basis_down,
    upward_own,
    downward_own,
    group_upward,
    nodes_skel,
    nodes,
    groups,
    node_mine,
    group_mine,
    near_sources,
    near_weights,
    near_targets,
    near_blocks,
    near_parts,
    far_sources,
    far_weights,
    far_targets,
    far_blocks,
    couple,
    near_codes_v,
    near_places_v,
    far_codes_v,
    near_codes,
    near_places,
    far_codes,
    load_sem,
    list_sem,
    halo_send,
    halo_recv,
    node_send,
    node_recv,
    group_send,
    group_recv,
):
    n_wide, n_narrow = lax.axis_size("wide"), lax.axis_size("narrow")
    g, n = lax.axis_index("wide"), lax.axis_index("narrow")
    leaves = leaf_links.shape[1]
    spare = 3 * leaves
    first_leaf = (g * n_narrow + n) * leaves - leaves
    at_end = (n == n_narrow - 1).astype(jnp.int32)
    at_start = (n == 0).astype(jnp.int32)
    after = (lax.rem(g + at_end, n_wide), lax.rem(n + 1, n_narrow))
    before = (
        lax.rem(g - at_start + n_wide, n_wide),
        lax.rem(n - 1 + n_narrow, n_narrow),
    )
    group_span = pl.ds(pl.multiple_of(g * (64 * n_narrow), 128), 64 * n_narrow)

    loads = []
    for k, (source, target) in enumerate(
        (
            (charges, c_own),
            (source_basis, basis_up),
            (leaf_upward, upward_own),
            (points, p_own),
            (leaf_skel, s_own),
            (node_upward.at[:, group_span], group_upward),
            (node_skel.at[:, group_span], nodes_skel),
            (leaf_downward, downward_own),
            (target_basis, basis_down),
        )
    ):
        copy = pltpu.make_async_copy(source, target, load_sem.at[k])
        copy.start()
        loads.append(copy)

    barrier = pltpu.get_barrier_semaphore()
    for device in (after, before):
        pl.semaphore_signal(barrier, inc=1, device_id=device, device_id_type=MESH)
    for step in range(1, n_narrow):
        pl.semaphore_signal(
            barrier, inc=1, device_id=(g, lax.rem(n + step, n_narrow)), device_id_type=MESH
        )
    for step in range(1, n_wide):
        pl.semaphore_signal(
            barrier, inc=1, device_id=(lax.rem(g + step, n_wide), n), device_id_type=MESH
        )
    pl.semaphore_wait(barrier, n_narrow + n_wide)

    def send(source, low, high, at):
        copies = []
        for target, device, k in ((low, after, 2 * at), (high, before, 2 * at + 1)):
            copy = pltpu.make_async_remote_copy(
                src_ref=source,
                dst_ref=target,
                send_sem=halo_send.at[k],
                recv_sem=halo_recv.at[k],
                device_id=device,
                device_id_type=MESH,
            )
            copy.start()
            copies.append(copy)
        return copies

    near_halo = send(points, p_low, p_high, 0) + send(charges, c_low, c_high, 1)

    codes, places, far = lists(near_list[...], leaf_links[...], first_leaf)
    near_codes_v[...], near_places_v[...], far_codes_v[...] = codes, places, far
    list_copies = []
    for k, (source, target) in enumerate(
        ((near_codes_v, near_codes), (near_places_v, near_places), (far_codes_v, far_codes))
    ):
        copy = pltpu.make_async_copy(source, target, list_sem.at[k])
        copy.start()
        list_copies.append(copy)

    for copy in loads[:3]:
        copy.wait()

    def upward(i, total):
        first = c_own[:, pl.ds(pl.multiple_of(i * 256, 256), 128)]
        second = c_own[:, pl.ds(pl.multiple_of(i * 256 + 128, 128), 128)]
        weights = jnp.concatenate([twice(first), twice(second)], axis=0)
        product = dot(weights, beside(basis_up[i]), NT)
        values = jnp.where(
            lane((16, 128)) < 64,
            product[0:16] + product[16:32],
            product[32:48] + product[48:64],
        )
        at = pl.ds(pl.multiple_of(i * 128, 128), 128)
        l_own[:, at] = values
        return total + dot(twice(values), beside(upward_own[:, at]), NT)

    total = lax.fori_loop(0, leaves // 2, upward, jnp.zeros((32, 64), F32), unroll=8)
    own = total[:16] + total[16:]
    node_mine[...] = jnp.concatenate([own, jnp.zeros_like(own)], axis=1)

    def gather(count, mine, table, device_of, place, send_sems, recv_sems):
        copies = []
        for step in range(1, count):
            copy = pltpu.make_async_remote_copy(
                src_ref=mine,
                dst_ref=table.at[place],
                send_sem=send_sems.at[step],
                recv_sem=recv_sems.at[step],
                device_id=device_of(step),
                device_id_type=MESH,
            )
            copy.start()
            copies.append(copy)
        table[place] = mine[...]
        return copies

    node_copies = gather(
        n_narrow, node_mine, nodes, lambda step: (g, lax.rem(n + step, n_narrow)), n, node_send, node_recv
    )
    far_halo = send(leaf_skel, s_low, s_high, 2) + send(l_own, l_low, l_high, 3)

    zero_rows = [jnp.zeros((8, 128), F32)] * 6
    for table in (near_sources, far_sources):
        parts = [source_parts(v) for v in source_values(zero_rows)]
        table[spare] = jnp.concatenate(parts, axis=1)
    for table in (near_weights, far_weights):
        table[spare] = jnp.zeros(table.shape[1:], BF16)

    def prepare_near(side, points_ref, charges_ref):
        def body(i, carry):
            start = pl.multiple_of(i * 128, 128)
            rows = source_tile(points_ref, start, 128)
            parts = [source_parts(v) for v in source_values(rows)]
            near_sources[side * leaves + i] = jnp.concatenate(parts, axis=1)
            near_weights[side * leaves + i] = twice(charges_ref[:, pl.ds(start, 128)])
            if side == 1:
                near_targets[i] = target_parts(rows)
            return carry

        lax.fori_loop(0, leaves, body, 0, unroll=4)

    def both_halves(x):
        low = lane(x.shape) < 64
        turned = pltpu.roll(x, 64, 1)
        return jnp.where(low, x, turned), jnp.where(low, turned, x)

    def prepare_far(side, points_ref, charges_ref):
        def body(i, carry):
            start = pl.multiple_of(i * 128, 128)
            rows = source_tile(points_ref, start, 128)
            split = [both_halves(v) for v in source_values(rows)]
            weights = both_halves(charges_ref[:, pl.ds(start, 128)])
            for k in range(2):
                parts = [source_parts(v[k]) for v in split]
                far_sources[side * leaves + 2 * i + k] = jnp.concatenate(parts, axis=1)
                far_weights[side * leaves + 2 * i + k] = twice(weights[k])
            if side == 1:
                targets = target_parts(rows)
                far_targets[2 * i] = targets[:64]
                far_targets[2 * i + 1] = targets[64:]
            return carry

        lax.fori_loop(0, leaves // 2, body, 0, unroll=4)

    def stream(count, first, second):
        first(0)

        def body(i, carry):
            second(i - 1)
            first(i)
            return carry

        lax.fori_loop(1, count, body, 0)
        second(count - 1)

    loads[3].wait()
    prepare_near(1, p_own, c_own)

    def self_first(i):
        for k in range(NEAR_STEP):
            leaf = i * NEAR_STEP + k
            near_blocks[k] = kernel_block(near_targets[leaf], near_sources[leaves + leaf])

    def self_second(i):
        for k in range(NEAR_STEP):
            leaf = i * NEAR_STEP + k
            sums = dot(near_weights[leaves + leaf], near_blocks[k], NT)
            near_out[:, pl.ds(pl.multiple_of(leaf * 128, 128), 128)] = sums[:16] + sums[16:]

    stream(leaves // NEAR_STEP, self_first, self_second)

    loads[4].wait()
    prepare_far(1, s_own, l_own)

    for copy in node_copies:
        copy.wait()
    loads[5].wait()
    group = dot(
        twice(jnp.concatenate(in_pairs(nodes, n_narrow), axis=1)), beside(group_upward[...]), NT
    )
    group = group[:16] + group[16:]
    group_mine[...] = jnp.concatenate([group, jnp.zeros_like(group)], axis=1)
    group_copies = gather(
        n_wide, group_mine, groups, lambda step: (lax.rem(g + step, n_wide), n), g, group_send, group_recv
    )

    for copy in list_copies:
        copy.wait()
    for copy in near_halo:
        copy.wait()
    prepare_near(0, p_low, c_low)
    prepare_near(2, p_high, c_high)

    def near_code(i, k):
        code = near_codes[0, i * NEAR_STEP + k]
        return code // 1024, lax.rem(code, 1024)

    def near_first(i):
        for k in range(NEAR_STEP):
            t, s = near_code(i, k)
            near_blocks[k] = kernel_block(near_targets[t], near_sources[s])

    def near_second(i):
        for k in range(NEAR_STEP):
            _, s = near_code(i, k)
            sums = dot(near_weights[s], near_blocks[k], NT)
            near_parts[i * NEAR_STEP + k] = sums[:16] + sums[16:]

    stream(NEAR_REST // NEAR_STEP, near_first, near_second)
    near_parts[NEAR_REST] = jnp.zeros((16, 128), F32)

    for copy in far_halo:
        copy.wait()
    prepare_far(0, s_low, l_low)
    prepare_far(2, s_high, l_high)

    low_s = (lax.rem(lane((48, 256)), 128) < 64).astype(F32).astype(BF16)
    high_s = jnp.ones_like(low_s) - low_s
    low_w, high_w = low_s[:32], high_s[:32]
    far_slots = leaf_links.shape[0]

    def far_picks(i):
        for k in range(FAR_STEP):
            for slot in range(0, far_slots, 2):
                leaf = FAR_STEP * i + k
                yield k, slot // 2, leaf, far_codes[slot, leaf], far_codes[slot + 1, leaf]

    def far_first(i):
        for k, j, leaf, a, b in far_picks(i):
            sources = far_sources[a] * low_s + far_sources[b] * high_s
            far_blocks[k * (far_slots // 2) + j] = kernel_block(far_targets[leaf], sources)

    def far_second(i):
        sums = [jnp.zeros((32, 64), F32)] * FAR_STEP
        for k, j, _, a, b in far_picks(i):
            weights = far_weights[a] * low_w + far_weights[b] * high_w
            sums[k] = sums[k] + dot(weights, far_blocks[k * (far_slots // 2) + j], NT)
        sums = [x[:16] + x[16:] for x in sums]
        for k in range(0, FAR_STEP, 2):
            at = pl.ds(pl.multiple_of((FAR_STEP * i + k) * 64, 128), 128)
            couple[:, at] = jnp.concatenate(sums[k : k + 2], axis=1)

    stream(leaves // FAR_STEP, far_first, far_second)

    for copy in group_copies:
        copy.wait()
    loads[6].wait()

    def half_of(skel, start, which):
        tile = source_tile(skel, pl.multiple_of(start, 128), 128)
        at = row((8, 128))
        values = jnp.where(at == 0, tile[0], jnp.where(at == 1, tile[1], tile[2]))
        values = jnp.where(which == 0, values, pltpu.roll(values, 64, 1))
        return values.T[:64]

    def marked(links, base, count):
        at = lane((1, 64 * count)) // 64
        hit = at < 0
        for k in range(links.shape[1]):
            hit = hit | (at == links[0, k] - base)
        return hit.astype(F32)

    def small(target, skel, values, mark):
        kernel = pair_kernel(target, skel) * mark
        sums = dot(twice(jnp.concatenate(values, axis=1)), beside(kernel), NT)
        return sums[:16] + sums[16:]

    group_fields = small(
        half_of(group_skel, (g // 2) * 128, lax.rem(g, 2)),
        group_skel[...],
        in_pairs(groups, n_wide),
        marked(group_links, 0, n_wide),
    )
    node_fields = dot(group_fields, node_downward[...], NN, HIGH) + small(
        half_of(nodes_skel, (n // 2) * 128, lax.rem(n, 2)),
        nodes_skel[...],
        in_pairs(nodes, n_narrow),
        marked(node_links, g * n_narrow, n_narrow),
    )
    field_halves = jnp.concatenate(halves(node_fields), axis=0)

    loads[7].wait()
    loads[8].wait()

    def downward(i, carry):
        at = pl.ds(pl.multiple_of(i * 128, 128), 128)
        product = dot(field_halves, beside(downward_own[:, at]), NN)
        fields = product[:16, :128] + product[16:, :128] + product[:16, 128:] + couple[:, at]
        low = lane((16, 128)) < 64
        lefts = [jnp.where(low, fields, 0.0), jnp.where(low, 0.0, fields)]
        left = jnp.concatenate([h for x in lefts for h in halves(x)], axis=0)
        product = dot(left, beside(basis_down[i]), NN)
        for k in range(2):
            leaf = 2 * i + k
            rows = product[32 * k : 32 * (k + 1)]
            value = rows[:16, :128] + rows[16:, :128] + rows[:16, 128:]
            for slot in range(1, near_list.shape[0]):
                value = value + near_parts[near_places[slot, leaf]]
            span = pl.ds(pl.multiple_of(leaf * 128, 128), 128)
            far_out[:, span] = value
        return carry

    lax.fori_loop(0, leaves // 2, downward, 0, unroll=4)


def on_device(
    points,
    charges,
    leaf_skel,
    node_skel,
    group_skel,
    source_basis,
    target_basis,
    leaf_upward,
    leaf_downward,
    node_upward,
    node_downward,
    near_list,
    leaf_links,
    node_links,
    group_links,
):
    n_wide, n_narrow = lax.axis_size("wide"), lax.axis_size("narrow")
    leaves, rank, size = source_basis.shape
    vmem = pl.BlockSpec(memory_space=pltpu.VMEM)
    smem = pl.BlockSpec(memory_space=pltpu.SMEM)
    anywhere = pl.BlockSpec(memory_space=pl.ANY)
    tables = 3 * leaves + 1
    table = (16, 128)
    paired = (leaves // 2, 2 * rank, size)

    def f32(*shape):
        return pltpu.VMEM(shape, F32)

    def bf16(*shape):
        return pltpu.VMEM(shape, BF16)

    def sems(count):
        return pltpu.SemaphoreType.DMA((count,))

    near, far = pl.pallas_call(
        fused,
        out_shape=[jax.ShapeDtypeStruct(charges.shape, F32)] * 2,
        in_specs=[vmem] * 2 + [smem] * 2 + [anywhere] * 9 + [vmem] * 2,
        out_specs=[vmem] * 2,
        scratch_shapes=[
            *[f32(*points.shape)] * 3,
            *[f32(*charges.shape)] * 3,
            *[f32(*leaf_skel.shape)] * 3,
            *[f32(16, leaf_skel.shape[1])] * 3,
            f32(*paired),
            f32(*paired),
            f32(*leaf_upward.shape),
            f32(*leaf_downward.shape),
            f32(64, 64 * n_narrow),
            f32(6, 64 * n_narrow),
            f32(n_narrow, *table),
            f32(n_wide, *table),
            f32(*table),
            f32(*table),
            bf16(tables, 48, 256),
            bf16(tables, 32, 256),
            bf16(leaves, 128, 48),
            bf16(NEAR_STEP, 128, 256),
            f32(NEAR_REST + 1, *table),
            bf16(tables, 48, 256),
            bf16(tables, 32, 256),
            bf16(leaves, 64, 48),
            bf16(4 * FAR_STEP, 64, 256),
            f32(16, leaf_skel.shape[1]),
            pltpu.VMEM((1, 256), jnp.int32),
            pltpu.VMEM((8, 128), jnp.int32),
            pltpu.VMEM((8, 128), jnp.int32),
            pltpu.SMEM((1, 256), jnp.int32),
            pltpu.SMEM((8, 128), jnp.int32),
            pltpu.SMEM((8, 128), jnp.int32),
            sems(9),
            sems(3),
            sems(8),
            sems(8),
            sems(n_narrow),
            sems(n_narrow),
            sems(n_wide),
            sems(n_wide),
        ],
        compiler_params=pltpu.CompilerParams(
            collective_id=0, has_side_effects=True, vmem_limit_bytes=VMEM_LIMIT
        ),
        name="fused",
    )(
        near_list.T,
        leaf_links.T,
        node_links,
        group_links,
        points,
        charges,
        leaf_skel,
        source_basis.reshape(paired),
        leaf_upward,
        node_upward,
        node_skel,
        target_basis.reshape(paired),
        leaf_downward,
        node_downward,
        group_skel,
    )
    return near + far


def solution(mesh):
    both = ("wide", "narrow")
    in_specs = (
        P(None, both),
        P(None, both),
        P(None, both),
        P(),
        P(),
        P(both, None, None),
        P(both, None, None),
        P(None, both),
        P(None, both),
        P(),
        P(None, both),
        P(both, None),
        P(both, None),
        P(both, None),
        P("wide", None),
    )
    return jax.shard_map(
        on_device, mesh=mesh, in_specs=in_specs, out_specs=P(None, both), check_vma=False
    )
```

```python
import math

import jax
import jax.numpy as jnp
from jax import lax
from jax.experimental import pallas as pl
from jax.experimental.pallas import tpu as pltpu
from jax.sharding import PartitionSpec as P

MESH = pl.DeviceIdType.MESH
HIGH = lax.Precision.HIGHEST
F32, BF16 = jnp.float32, jnp.bfloat16
SMOOTH = 0.25
COEFFICIENT = 1.0 / (4.0 * math.pi)
NT = (((1,), (1,)), ((), ()))
NN = (((1,), (0,)), ((), ()))
NEAR_REST = 288 - 64
NEAR_STEP = 32
FAR_STEP = 8
FINISH_STEPS = 4
VMEM_LIMIT = 56 * 2**20


def dot(a, b, dims, precision=None):
    return lax.dot_general(a, b, dims, precision=precision, preferred_element_type=F32)


def halves(x):
    high = x.astype(BF16)
    return high, (x - high.astype(F32)).astype(BF16)


def twice(x):
    high, low = halves(x)
    stacked = jnp.concatenate([high, low], axis=0)
    return jnp.concatenate([stacked, stacked], axis=1)


def beside(x):
    high, low = halves(x)
    return jnp.concatenate([high, low], axis=1)


def pieces(x):
    first = x.astype(BF16).astype(F32)
    rest = x - first
    second = rest.astype(BF16).astype(F32)
    return first, second, rest - second


def lane(shape):
    return lax.broadcasted_iota(jnp.int32, shape, 1)


def row(shape):
    return lax.broadcasted_iota(jnp.int32, shape, 0)


def in_pairs(ref, count):
    return [
        ref[2 * i] + pltpu.roll(ref[2 * i + 1], 64, 1) for i in range(count // 2)
    ]


def source_tile(ref, start, width):
    return [
        jnp.broadcast_to(ref[k : k + 1, pl.ds(start, width)], (8, width)) for k in range(6)
    ]


def source_values(rows):
    y0, y1, y2, m0, m1, m2 = rows
    at = row(y0.shape)
    square = y0 * y0 + y1 * y1 + y2 * y2 + SMOOTH
    flux = (y0 * m0 + y1 * m1 + y2 * m2) * (-COEFFICIENT)
    one, zero = jnp.ones_like(y0), jnp.zeros_like(y0)

    def pick(*terms):
        out = zero
        for k in reversed(range(len(terms))):
            out = jnp.where(at == k, terms[k], out)
        return out

    return (
        pick(-2.0 * y0, -2.0 * y1, -2.0 * y2, square, one),
        pick(COEFFICIENT * m0, COEFFICIENT * m1, COEFFICIENT * m2, flux),
    )


def source_parts(values):
    first, second, third = pieces(values)
    return jnp.concatenate([first, second, third, first, second, first], axis=0).astype(BF16)


def target_parts(rows):
    x0, x1, x2 = rows[:3]
    at = row(x0.shape)
    square = x0 * x0 + x1 * x1 + x2 * x2
    values = jnp.where(at == 0, x0, jnp.where(at == 1, x1, jnp.where(at == 2, x2, 0.0)))
    values = jnp.where(at == 3, 1.0, jnp.where(at == 4, square, values))
    first, second, third = pieces(values)
    fill = jnp.zeros((80, values.shape[1]), F32)
    stacked = jnp.concatenate([first, first, first, second, second, third, fill], axis=0)
    return stacked.T.astype(BF16)[:, :48]


def kernel_block(targets, sources):
    both = dot(targets, sources, NN)
    width = both.shape[1] // 2
    root = lax.rsqrt(both[:, :width])
    return beside((both[:, width:] * root) * (root * root))


def pair_kernel(target, source):
    offset = [target[:, k : k + 1] - source[k : k + 1] for k in range(3)]
    distance = offset[0] * offset[0] + offset[1] * offset[1] + offset[2] * offset[2] + SMOOTH
    flux = offset[0] * source[3:4] + offset[1] * source[4:5] + offset[2] * source[5:6]
    root = lax.rsqrt(distance)
    return (flux * root) * (root * root) * COEFFICIENT


def lists(near, links, first_leaf):
    slots, leaves = near.shape
    fill = jnp.full((slots, 128 - leaves), -1, jnp.int32)
    near = jnp.concatenate([near, fill], axis=1)
    links = jnp.concatenate([links, fill], axis=1)
    spare = 3 * leaves
    far = jnp.where(links < 0, spare, jnp.clip(links - first_leaf, 0, spare - 1))
    across, down = lane(near.shape), row(near.shape)
    used = (near >= 0) & (down > 0)
    count = used.astype(jnp.int32)
    along = count
    step = 1
    while step < leaves:
        along = along + jnp.where(across >= step, pltpu.roll(along, step, 1), 0)
        step *= 2
    totals = jnp.broadcast_to(along[:, leaves - 1 : leaves], along.shape)
    above = totals
    step = 1
    while step < slots:
        above = above + jnp.where(down >= step, pltpu.roll(above, step, 0), 0)
        step *= 2
    place = along - count + above - totals
    place = jnp.where(used, jnp.minimum(place, NEAR_REST), NEAR_REST)
    code = across * 1024 + jnp.clip(near - first_leaf, 0, spare - 1) + 1
    places, codes = place.T[:leaves], code.T[:leaves]
    at = lane((leaves, 256))
    hits = jnp.zeros((leaves, 256), jnp.int32)
    for slot in range(1, slots):
        hits = hits + jnp.where(places[:, slot : slot + 1] == at, codes[:, slot : slot + 1], 0)
    packed = jnp.sum(hits, axis=0, keepdims=True)
    return jnp.where((packed > 0) & (lane((1, 256)) < NEAR_REST), packed - 1, spare), place, far


def fused(
    near_list,
    leaf_links,
    node_links,
    group_links,
    points,
    charges,
    leaf_skel,
    source_basis,
    leaf_upward,
    node_upward,
    node_skel,
    node_downward,
    group_skel,
    near,
    couple,
    fields,
    p_low,
    p_own,
    p_high,
    c_low,
    c_own,
    c_high,
    s_low,
    s_own,
    s_high,
    l_low,
    l_own,
    l_high,
    basis_up,
    upward_own,
    group_upward,
    nodes_skel,
    nodes,
    groups,
    node_mine,
    group_mine,
    near_sources,
    near_weights,
    near_targets,
    near_blocks,
    near_parts,
    far_sources,
    far_weights,
    far_targets,
    far_blocks,
    near_codes_v,
    near_places_v,
    far_codes_v,
    near_codes,
    near_places,
    far_codes,
    load_sem,
    list_sem,
    halo_send,
    halo_recv,
    node_send,
    node_recv,
    group_send,
    group_recv,
):
    n_wide, n_narrow = lax.axis_size("wide"), lax.axis_size("narrow")
    g, n = lax.axis_index("wide"), lax.axis_index("narrow")
    leaves = leaf_links.shape[1]
    spare = 3 * leaves
    first_leaf = (g * n_narrow + n) * leaves - leaves
    at_end = (n == n_narrow - 1).astype(jnp.int32)
    at_start = (n == 0).astype(jnp.int32)
    after = (lax.rem(g + at_end, n_wide), lax.rem(n + 1, n_narrow))
    before = (
        lax.rem(g - at_start + n_wide, n_wide),
        lax.rem(n - 1 + n_narrow, n_narrow),
    )
    group_span = pl.ds(pl.multiple_of(g * (64 * n_narrow), 128), 64 * n_narrow)

    loads = []
    for k, (source, target) in enumerate(
        (
            (charges, c_own),
            (source_basis, basis_up),
            (leaf_upward, upward_own),
            (points, p_own),
            (leaf_skel, s_own),
            (node_upward.at[:, group_span], group_upward),
            (node_skel.at[:, group_span], nodes_skel),
        )
    ):
        copy = pltpu.make_async_copy(source, target, load_sem.at[k])
        copy.start()
        loads.append(copy)

    barrier = pltpu.get_barrier_semaphore()
    for device in (after, before):
        pl.semaphore_signal(barrier, inc=1, device_id=device, device_id_type=MESH)
    for step in range(1, n_narrow):
        pl.semaphore_signal(
            barrier, inc=1, device_id=(g, lax.rem(n + step, n_narrow)), device_id_type=MESH
        )
    for step in range(1, n_wide):
        pl.semaphore_signal(
            barrier, inc=1, device_id=(lax.rem(g + step, n_wide), n), device_id_type=MESH
        )
    pl.semaphore_wait(barrier, n_narrow + n_wide)

    def send(source, low, high, at):
        copies = []
        for target, device, k in ((low, after, 2 * at), (high, before, 2 * at + 1)):
            copy = pltpu.make_async_remote_copy(
                src_ref=source,
                dst_ref=target,
                send_sem=halo_send.at[k],
                recv_sem=halo_recv.at[k],
                device_id=device,
                device_id_type=MESH,
            )
            copy.start()
            copies.append(copy)
        return copies

    near_halo = send(points, p_low, p_high, 0)
    far_halo = send(leaf_skel, s_low, s_high, 2)

    codes, places, far = lists(near_list[...], leaf_links[...], first_leaf)
    near_codes_v[...], near_places_v[...], far_codes_v[...] = codes, places, far
    list_copies = []
    for k, (source, target) in enumerate(
        ((near_codes_v, near_codes), (near_places_v, near_places), (far_codes_v, far_codes))
    ):
        copy = pltpu.make_async_copy(source, target, list_sem.at[k])
        copy.start()
        list_copies.append(copy)

    for copy in loads[:3]:
        copy.wait()

    def upward(i, total):
        first = c_own[:, pl.ds(pl.multiple_of(i * 256, 256), 128)]
        second = c_own[:, pl.ds(pl.multiple_of(i * 256 + 128, 128), 128)]
        weights = jnp.concatenate([twice(first), twice(second)], axis=0)
        product = dot(weights, beside(basis_up[i]), NT)
        values = jnp.where(
            lane((16, 128)) < 64,
            product[0:16] + product[16:32],
            product[32:48] + product[48:64],
        )
        at = pl.ds(pl.multiple_of(i * 128, 128), 128)
        l_own[:, at] = values
        return total + dot(twice(values), beside(upward_own[:, at]), NT)

    total = lax.fori_loop(0, leaves // 2, upward, jnp.zeros((32, 64), F32), unroll=8)
    own = total[:16] + total[16:]
    node_mine[...] = jnp.concatenate([own, jnp.zeros_like(own)], axis=1)

    def gather(count, mine, table, device_of, place, send_sems, recv_sems):
        copies = []
        for step in range(1, count):
            copy = pltpu.make_async_remote_copy(
                src_ref=mine,
                dst_ref=table.at[place],
                send_sem=send_sems.at[step],
                recv_sem=recv_sems.at[step],
                device_id=device_of(step),
                device_id_type=MESH,
            )
            copy.start()
            copies.append(copy)
        table[place] = mine[...]
        return copies

    node_copies = gather(
        n_narrow, node_mine, nodes, lambda step: (g, lax.rem(n + step, n_narrow)), n, node_send, node_recv
    )
    far_halo += send(l_own, l_low, l_high, 3)
    near_halo += send(charges, c_low, c_high, 1)

    zero_rows = [jnp.zeros((8, 128), F32)] * 6
    for table in (near_sources, far_sources):
        parts = [source_parts(v) for v in source_values(zero_rows)]
        table[spare] = jnp.concatenate(parts, axis=1)
    for table in (near_weights, far_weights):
        table[spare] = jnp.zeros(table.shape[1:], BF16)

    def prepare_near(side, points_ref, charges_ref):
        def body(i, carry):
            start = pl.multiple_of(i * 128, 128)
            rows = source_tile(points_ref, start, 128)
            parts = [source_parts(v) for v in source_values(rows)]
            near_sources[side * leaves + i] = jnp.concatenate(parts, axis=1)
            near_weights[side * leaves + i] = twice(charges_ref[:, pl.ds(start, 128)])
            if side == 1:
                near_targets[i] = target_parts(rows)
            return carry

        lax.fori_loop(0, leaves, body, 0, unroll=4)

    def both_halves(x):
        low = lane(x.shape) < 64
        turned = pltpu.roll(x, 64, 1)
        return jnp.where(low, x, turned), jnp.where(low, turned, x)

    def prepare_far(side, points_ref, charges_ref):
        def body(i, carry):
            start = pl.multiple_of(i * 128, 128)
            rows = source_tile(points_ref, start, 128)
            split = [both_halves(v) for v in source_values(rows)]
            weights = both_halves(charges_ref[:, pl.ds(start, 128)])
            for k in range(2):
                parts = [source_parts(v[k]) for v in split]
                far_sources[side * leaves + 2 * i + k] = jnp.concatenate(parts, axis=1)
                far_weights[side * leaves + 2 * i + k] = twice(weights[k])
            if side == 1:
                targets = target_parts(rows)
                far_targets[2 * i] = targets[:64]
                far_targets[2 * i + 1] = targets[64:]
            return carry

        lax.fori_loop(0, leaves // 2, body, 0, unroll=4)

    def stream(count, first, second):
        first(0)

        def body(i, carry):
            second(i - 1)
            first(i)
            return carry

        lax.fori_loop(1, count, body, 0)
        second(count - 1)

    loads[3].wait()
    prepare_near(1, p_own, c_own)

    def self_first(i):
        for k in range(NEAR_STEP):
            leaf = i * NEAR_STEP + k
            near_blocks[k] = kernel_block(near_targets[leaf], near_sources[leaves + leaf])

    def self_second(i):
        for k in range(NEAR_STEP):
            leaf = i * NEAR_STEP + k
            sums = dot(near_weights[leaves + leaf], near_blocks[k], NT)
            near[:, pl.ds(pl.multiple_of(leaf * 128, 128), 128)] = sums[:16] + sums[16:]

    stream(leaves // NEAR_STEP, self_first, self_second)

    loads[4].wait()
    prepare_far(1, s_own, l_own)

    for copy in node_copies:
        copy.wait()
    loads[5].wait()
    group = dot(
        twice(jnp.concatenate(in_pairs(nodes, n_narrow), axis=1)), beside(group_upward[...]), NT
    )
    group = group[:16] + group[16:]
    group_mine[...] = jnp.concatenate([group, jnp.zeros_like(group)], axis=1)
    group_copies = gather(
        n_wide, group_mine, groups, lambda step: (lax.rem(g + step, n_wide), n), g, group_send, group_recv
    )

    for copy in list_copies:
        copy.wait()
    for copy in far_halo:
        copy.wait()
    prepare_far(0, s_low, l_low)
    prepare_far(2, s_high, l_high)

    low_s = (lax.rem(lane((48, 256)), 128) < 64).astype(F32).astype(BF16)
    high_s = jnp.ones_like(low_s) - low_s
    low_w, high_w = low_s[:32], high_s[:32]
    far_slots = leaf_links.shape[0]

    def far_picks(i):
        for k in range(FAR_STEP):
            for slot in range(0, far_slots, 2):
                leaf = FAR_STEP * i + k
                yield k, slot // 2, leaf, far_codes[slot, leaf], far_codes[slot + 1, leaf]

    def far_first(i):
        for k, j, leaf, a, b in far_picks(i):
            sources = far_sources[a] * low_s + far_sources[b] * high_s
            far_blocks[k * (far_slots // 2) + j] = kernel_block(far_targets[leaf], sources)

    def far_second(i):
        sums = [jnp.zeros((32, 64), F32)] * FAR_STEP
        for k, j, _, a, b in far_picks(i):
            weights = far_weights[a] * low_w + far_weights[b] * high_w
            sums[k] = sums[k] + dot(weights, far_blocks[k * (far_slots // 2) + j], NT)
        sums = [x[:16] + x[16:] for x in sums]
        for k in range(0, FAR_STEP, 2):
            at = pl.ds(pl.multiple_of((FAR_STEP * i + k) * 64, 128), 128)
            couple[:, at] = jnp.concatenate(sums[k : k + 2], axis=1)

    stream(leaves // FAR_STEP, far_first, far_second)

    for copy in near_halo:
        copy.wait()
    prepare_near(0, p_low, c_low)
    prepare_near(2, p_high, c_high)

    def near_code(i, k):
        code = near_codes[0, i * NEAR_STEP + k]
        return code // 1024, lax.rem(code, 1024)

    def near_first(i):
        for k in range(NEAR_STEP):
            t, s = near_code(i, k)
            near_blocks[k] = kernel_block(near_targets[t], near_sources[s])

    def near_second(i):
        for k in range(NEAR_STEP):
            _, s = near_code(i, k)
            sums = dot(near_weights[s], near_blocks[k], NT)
            near_parts[i * NEAR_STEP + k] = sums[:16] + sums[16:]

    stream(NEAR_REST // NEAR_STEP, near_first, near_second)
    near_parts[NEAR_REST] = jnp.zeros((16, 128), F32)

    for copy in group_copies:
        copy.wait()
    loads[6].wait()

    def half_of(skel, start, which):
        tile = source_tile(skel, pl.multiple_of(start, 128), 128)
        at = row((8, 128))
        values = jnp.where(at == 0, tile[0], jnp.where(at == 1, tile[1], tile[2]))
        values = jnp.where(which == 0, values, pltpu.roll(values, 64, 1))
        return values.T[:64]

    def marked(links, base, count):
        at = lane((1, 64 * count)) // 64
        hit = at < 0
        for k in range(links.shape[1]):
            hit = hit | (at == links[0, k] - base)
        return hit.astype(F32)

    def small(target, skel, values, mark):
        kernel = pair_kernel(target, skel) * mark
        sums = dot(twice(jnp.concatenate(values, axis=1)), beside(kernel), NT)
        return sums[:16] + sums[16:]

    group_fields = small(
        half_of(group_skel, (g // 2) * 128, lax.rem(g, 2)),
        group_skel[...],
        in_pairs(groups, n_wide),
        marked(group_links, 0, n_wide),
    )
    node_fields = dot(group_fields, node_downward[...], NN, HIGH) + small(
        half_of(nodes_skel, (n // 2) * 128, lax.rem(n, 2)),
        nodes_skel[...],
        in_pairs(nodes, n_narrow),
        marked(node_links, g * n_narrow, n_narrow),
    )
    fields[...] = node_fields

    def collect(leaf, carry):
        span = pl.ds(pl.multiple_of(leaf * 128, 128), 128)
        value = near[:, span]
        for slot in range(1, near_list.shape[0]):
            value = value + near_parts[near_places[slot, leaf]]
        near[:, span] = value
        return carry

    lax.fori_loop(0, leaves, collect, 0, unroll=8)


def finish(fields, near, couple, leaf_downward, basis, out):
    field_halves = jnp.concatenate(halves(fields[...]), axis=0)
    low = lane((16, 128)) < 64
    for i in range(basis.shape[0]):
        at = slice(128 * i, 128 * (i + 1))
        product = dot(field_halves, beside(leaf_downward[:, at]), NN)
        leaf = product[:16, :128] + product[16:, :128] + product[:16, 128:] + couple[:, at]
        lefts = [jnp.where(low, leaf, 0.0), jnp.where(low, 0.0, leaf)]
        left = jnp.concatenate([h for x in lefts for h in halves(x)], axis=0)
        product = dot(left, beside(basis[i]), NN)
        for k in range(2):
            rows = product[32 * k : 32 * (k + 1)]
            span = slice(256 * i + 128 * k, 256 * i + 128 * (k + 1))
            out[:, span] = near[:, span] + (rows[:16, :128] + rows[16:, :128] + rows[:16, 128:])


def on_device(
    points,
    charges,
    leaf_skel,
    node_skel,
    group_skel,
    source_basis,
    target_basis,
    leaf_upward,
    leaf_downward,
    node_upward,
    node_downward,
    near_list,
    leaf_links,
    node_links,
    group_links,
):
    n_wide, n_narrow = lax.axis_size("wide"), lax.axis_size("narrow")
    leaves, rank, size = source_basis.shape
    vmem = pl.BlockSpec(memory_space=pltpu.VMEM)
    smem = pl.BlockSpec(memory_space=pltpu.SMEM)
    anywhere = pl.BlockSpec(memory_space=pl.ANY)
    tables = 3 * leaves + 1
    table = (16, 128)
    paired = (leaves // 2, 2 * rank, size)

    def f32(*shape):
        return pltpu.VMEM(shape, F32)

    def bf16(*shape):
        return pltpu.VMEM(shape, BF16)

    def sems(count):
        return pltpu.SemaphoreType.DMA((count,))

    near, couple, fields = pl.pallas_call(
        fused,
        out_shape=[
            jax.ShapeDtypeStruct(charges.shape, F32),
            jax.ShapeDtypeStruct((16, leaf_skel.shape[1]), F32),
            jax.ShapeDtypeStruct((16, rank), F32),
        ],
        in_specs=[vmem] * 2 + [smem] * 2 + [anywhere] * 7 + [vmem] * 2,
        out_specs=[vmem] * 3,
        scratch_shapes=[
            *[f32(*points.shape)] * 3,
            *[f32(*charges.shape)] * 3,
            *[f32(*leaf_skel.shape)] * 3,
            *[f32(16, leaf_skel.shape[1])] * 3,
            f32(*paired),
            f32(*leaf_upward.shape),
            f32(64, 64 * n_narrow),
            f32(6, 64 * n_narrow),
            f32(n_narrow, *table),
            f32(n_wide, *table),
            f32(*table),
            f32(*table),
            bf16(tables, 48, 256),
            bf16(tables, 32, 256),
            bf16(leaves, 128, 48),
            bf16(NEAR_STEP, 128, 256),
            f32(NEAR_REST + 1, *table),
            bf16(tables, 48, 256),
            bf16(tables, 32, 256),
            bf16(leaves, 64, 48),
            bf16(4 * FAR_STEP, 64, 256),
            pltpu.VMEM((1, 256), jnp.int32),
            pltpu.VMEM((8, 128), jnp.int32),
            pltpu.VMEM((8, 128), jnp.int32),
            pltpu.SMEM((1, 256), jnp.int32),
            pltpu.SMEM((8, 128), jnp.int32),
            pltpu.SMEM((8, 128), jnp.int32),
            sems(7),
            sems(3),
            sems(8),
            sems(8),
            sems(n_narrow),
            sems(n_narrow),
            sems(n_wide),
            sems(n_wide),
        ],
        compiler_params=pltpu.CompilerParams(
            collective_id=0, has_side_effects=True, vmem_limit_bytes=VMEM_LIMIT
        ),
        name="fused",
    )(
        near_list.T,
        leaf_links.T,
        node_links,
        group_links,
        points,
        charges,
        leaf_skel,
        source_basis.reshape(paired),
        leaf_upward,
        node_upward,
        node_skel,
        node_downward,
        group_skel,
    )
    steps = FINISH_STEPS

    def columns(rows, total):
        return pl.BlockSpec((rows, total // steps), lambda i: (0, i))

    return pl.pallas_call(
        finish,
        grid=(steps,),
        out_shape=jax.ShapeDtypeStruct(charges.shape, F32),
        in_specs=[
            pl.BlockSpec(fields.shape, lambda i: (0, 0)),
            columns(*near.shape),
            columns(*couple.shape),
            columns(*leaf_downward.shape),
            pl.BlockSpec((paired[0] // steps, *paired[1:]), lambda i: (i, 0, 0)),
        ],
        out_specs=columns(*near.shape),
        name="finish",
    )(fields, near, couple, leaf_downward, target_basis.reshape(paired))


def solution(mesh):
    both = ("wide", "narrow")
    in_specs = (
        P(None, both),
        P(None, both),
        P(None, both),
        P(),
        P(),
        P(both, None, None),
        P(both, None, None),
        P(None, both),
        P(None, both),
        P(),
        P(None, both),
        P(both, None),
        P(both, None),
        P(both, None),
        P("wide", None),
    )
    return jax.shard_map(
        on_device, mesh=mesh, in_specs=in_specs, out_specs=P(None, both), check_vma=False
    )
```

```python
import math

import jax
import jax.numpy as jnp
from jax import lax
from jax.experimental import pallas as pl
from jax.experimental.pallas import tpu as pltpu
from jax.sharding import PartitionSpec as P

MESH = pl.DeviceIdType.MESH
HIGH = lax.Precision.HIGHEST
F32, BF16 = jnp.float32, jnp.bfloat16
SMOOTH = 0.25
COEFFICIENT = 1.0 / (4.0 * math.pi)
NT = (((1,), (1,)), ((), ()))
NN = (((1,), (0,)), ((), ()))
NEAR_REST = 288 - 64
NEAR_STEP = 32
FAR_STEP = 8
FINISH_STEPS = 4
VMEM_LIMIT = 56 * 2**20


def dot(a, b, dims, precision=None):
    return lax.dot_general(a, b, dims, precision=precision, preferred_element_type=F32)


def halves(x):
    high = x.astype(BF16)
    return high, (x - high.astype(F32)).astype(BF16)


def twice(x):
    high, low = halves(x)
    stacked = jnp.concatenate([high, low], axis=0)
    return jnp.concatenate([stacked, stacked], axis=1)


def beside(x):
    high, low = halves(x)
    return jnp.concatenate([high, low], axis=1)


def pieces(x):
    first = x.astype(BF16).astype(F32)
    rest = x - first
    second = rest.astype(BF16).astype(F32)
    return first, second, rest - second


def lane(shape):
    return lax.broadcasted_iota(jnp.int32, shape, 1)


def row(shape):
    return lax.broadcasted_iota(jnp.int32, shape, 0)


def in_pairs(ref, count):
    return [
        ref[2 * i] + pltpu.roll(ref[2 * i + 1], 64, 1) for i in range(count // 2)
    ]


def source_tile(ref, start, width):
    return [
        jnp.broadcast_to(ref[k : k + 1, pl.ds(start, width)], (8, width)) for k in range(6)
    ]


def source_values(rows):
    y0, y1, y2, m0, m1, m2 = rows
    at = row(y0.shape)
    square = y0 * y0 + y1 * y1 + y2 * y2 + SMOOTH
    flux = (y0 * m0 + y1 * m1 + y2 * m2) * (-COEFFICIENT)
    one, zero = jnp.ones_like(y0), jnp.zeros_like(y0)

    def pick(*terms):
        out = zero
        for k in reversed(range(len(terms))):
            out = jnp.where(at == k, terms[k], out)
        return out

    return (
        pick(-2.0 * y0, -2.0 * y1, -2.0 * y2, square, one),
        pick(COEFFICIENT * m0, COEFFICIENT * m1, COEFFICIENT * m2, flux),
    )


def source_parts(values):
    first, second, third = pieces(values)
    return jnp.concatenate([first, second, third, first, second, first], axis=0).astype(BF16)


def target_parts(rows):
    x0, x1, x2 = rows[:3]
    at = row(x0.shape)
    square = x0 * x0 + x1 * x1 + x2 * x2
    values = jnp.where(at == 0, x0, jnp.where(at == 1, x1, jnp.where(at == 2, x2, 0.0)))
    values = jnp.where(at == 3, 1.0, jnp.where(at == 4, square, values))
    first, second, third = pieces(values)
    fill = jnp.zeros((80, values.shape[1]), F32)
    stacked = jnp.concatenate([first, first, first, second, second, third, fill], axis=0)
    return stacked.T.astype(BF16)[:, :48]


def kernel_block(targets, sources):
    both = dot(targets, sources, NN)
    width = both.shape[1] // 2
    root = lax.rsqrt(both[:, :width])
    return beside((both[:, width:] * root) * (root * root))


def pair_kernel(target, source):
    offset = [target[:, k : k + 1] - source[k : k + 1] for k in range(3)]
    distance = offset[0] * offset[0] + offset[1] * offset[1] + offset[2] * offset[2] + SMOOTH
    flux = offset[0] * source[3:4] + offset[1] * source[4:5] + offset[2] * source[5:6]
    root = lax.rsqrt(distance)
    return (flux * root) * (root * root) * COEFFICIENT


def lists(near, links, first_leaf):
    slots, leaves = near.shape
    fill = jnp.full((slots, 128 - leaves), -1, jnp.int32)
    near = jnp.concatenate([near, fill], axis=1)
    links = jnp.concatenate([links, fill], axis=1)
    spare = 3 * leaves
    far = jnp.where(links < 0, spare, jnp.clip(links - first_leaf, 0, spare - 1))
    across, down = lane(near.shape), row(near.shape)
    used = (near >= 0) & (down > 0)
    count = used.astype(jnp.int32)
    along = count
    step = 1
    while step < leaves:
        along = along + jnp.where(across >= step, pltpu.roll(along, step, 1), 0)
        step *= 2
    totals = jnp.broadcast_to(along[:, leaves - 1 : leaves], along.shape)
    above = totals
    step = 1
    while step < slots:
        above = above + jnp.where(down >= step, pltpu.roll(above, step, 0), 0)
        step *= 2
    place = along - count + above - totals
    place = jnp.where(used, jnp.minimum(place, NEAR_REST), NEAR_REST)
    code = across * 1024 + jnp.clip(near - first_leaf, 0, spare - 1) + 1
    places, codes = place.T[:leaves], code.T[:leaves]
    at = lane((leaves, 256))
    hits = jnp.zeros((leaves, 256), jnp.int32)
    for slot in range(1, slots):
        hits = hits + jnp.where(places[:, slot : slot + 1] == at, codes[:, slot : slot + 1], 0)
    packed = jnp.sum(hits, axis=0, keepdims=True)
    return jnp.where((packed > 0) & (lane((1, 256)) < NEAR_REST), packed - 1, spare), place, far


def fused(
    near_list,
    leaf_links,
    node_links,
    group_links,
    points,
    charges,
    leaf_skel,
    source_basis,
    leaf_upward,
    node_upward,
    node_skel,
    node_downward,
    group_skel,
    near,
    couple,
    fields,
    p_low,
    p_own,
    p_high,
    c_low,
    c_own,
    c_high,
    s_low,
    s_own,
    s_high,
    l_low,
    l_own,
    l_high,
    basis_up,
    upward_own,
    group_upward,
    nodes_skel,
    nodes,
    groups,
    node_mine,
    group_mine,
    near_sources,
    near_weights,
    near_targets,
    near_blocks,
    near_parts,
    far_sources,
    far_weights,
    far_targets,
    far_blocks,
    near_list_v,
    leaf_links_v,
    group_skel_v,
    node_downward_v,
    couple_v,
    near_codes_v,
    near_places_v,
    far_codes_v,
    near_codes,
    near_places,
    far_codes,
    load_sem,
    list_sem,
    halo_send,
    halo_recv,
    node_send,
    node_recv,
    group_send,
    group_recv,
):
    n_wide, n_narrow = lax.axis_size("wide"), lax.axis_size("narrow")
    g, n = lax.axis_index("wide"), lax.axis_index("narrow")
    leaves = leaf_links.shape[1]
    spare = 3 * leaves
    first_leaf = (g * n_narrow + n) * leaves - leaves
    at_end = (n == n_narrow - 1).astype(jnp.int32)
    at_start = (n == 0).astype(jnp.int32)
    after = (lax.rem(g + at_end, n_wide), lax.rem(n + 1, n_narrow))
    before = (
        lax.rem(g - at_start + n_wide, n_wide),
        lax.rem(n - 1 + n_narrow, n_narrow),
    )
    group_span = pl.ds(pl.multiple_of(g * (64 * n_narrow), 128), 64 * n_narrow)

    loads = []
    for k, (source, target) in enumerate(
        (
            (charges, c_own),
            (source_basis, basis_up),
            (leaf_upward, upward_own),
            (points, p_own),
            (near_list, near_list_v),
            (leaf_links, leaf_links_v),
            (leaf_skel, s_own),
            (node_upward.at[:, group_span], group_upward),
            (node_skel.at[:, group_span], nodes_skel),
            (group_skel, group_skel_v),
            (node_downward, node_downward_v),
        )
    ):
        copy = pltpu.make_async_copy(source, target, load_sem.at[k])
        copy.start()
        loads.append(copy)

    barrier = pltpu.get_barrier_semaphore()
    for device in (after, before):
        pl.semaphore_signal(barrier, inc=1, device_id=device, device_id_type=MESH)
    for step in range(1, n_narrow):
        pl.semaphore_signal(
            barrier, inc=1, device_id=(g, lax.rem(n + step, n_narrow)), device_id_type=MESH
        )
    for step in range(1, n_wide):
        pl.semaphore_signal(
            barrier, inc=1, device_id=(lax.rem(g + step, n_wide), n), device_id_type=MESH
        )

    def send(source, low, high, at):
        copies = []
        for target, device, k in ((low, after, 2 * at), (high, before, 2 * at + 1)):
            copy = pltpu.make_async_remote_copy(
                src_ref=source,
                dst_ref=target,
                send_sem=halo_send.at[k],
                recv_sem=halo_recv.at[k],
                device_id=device,
                device_id_type=MESH,
            )
            copy.start()
            copies.append(copy)
        return copies

    for copy in loads[:3]:
        copy.wait()

    def upward(i, total):
        first = c_own[:, pl.ds(pl.multiple_of(i * 256, 256), 128)]
        second = c_own[:, pl.ds(pl.multiple_of(i * 256 + 128, 128), 128)]
        weights = jnp.concatenate([twice(first), twice(second)], axis=0)
        product = dot(weights, beside(basis_up[i]), NT)
        values = jnp.where(
            lane((16, 128)) < 64,
            product[0:16] + product[16:32],
            product[32:48] + product[48:64],
        )
        at = pl.ds(pl.multiple_of(i * 128, 128), 128)
        l_own[:, at] = values
        return total + dot(twice(values), beside(upward_own[:, at]), NT)

    total = lax.fori_loop(0, leaves // 2, upward, jnp.zeros((32, 64), F32), unroll=8)
    own = total[:16] + total[16:]
    node_mine[...] = jnp.concatenate([own, jnp.zeros_like(own)], axis=1)

    zero_rows = [jnp.zeros((8, 128), F32)] * 6
    for table in (near_sources, far_sources):
        parts = [source_parts(v) for v in source_values(zero_rows)]
        table[spare] = jnp.concatenate(parts, axis=1)
    for table in (near_weights, far_weights):
        table[spare] = jnp.zeros(table.shape[1:], BF16)

    def prepare_near(side, points_ref, charges_ref):
        def body(i, carry):
            start = pl.multiple_of(i * 128, 128)
            rows = source_tile(points_ref, start, 128)
            parts = [source_parts(v) for v in source_values(rows)]
            near_sources[side * leaves + i] = jnp.concatenate(parts, axis=1)
            near_weights[side * leaves + i] = twice(charges_ref[:, pl.ds(start, 128)])
            if side == 1:
                near_targets[i] = target_parts(rows)
            return carry

        lax.fori_loop(0, leaves, body, 0, unroll=4)

    def both_halves(x):
        low = lane(x.shape) < 64
        turned = pltpu.roll(x, 64, 1)
        return jnp.where(low, x, turned), jnp.where(low, turned, x)

    def prepare_far(side, points_ref, charges_ref):
        def body(i, carry):
            start = pl.multiple_of(i * 128, 128)
            rows = source_tile(points_ref, start, 128)
            split = [both_halves(v) for v in source_values(rows)]
            weights = both_halves(charges_ref[:, pl.ds(start, 128)])
            for k in range(2):
                parts = [source_parts(v[k]) for v in split]
                far_sources[side * leaves + 2 * i + k] = jnp.concatenate(parts, axis=1)
                far_weights[side * leaves + 2 * i + k] = twice(weights[k])
            if side == 1:
                targets = target_parts(rows)
                far_targets[2 * i] = targets[:64]
                far_targets[2 * i + 1] = targets[64:]
            return carry

        lax.fori_loop(0, leaves // 2, body, 0, unroll=4)

    def stream(count, first, second):
        first(0)

        def body(i, carry):
            second(i - 1)
            first(i)
            return carry

        lax.fori_loop(1, count, body, 0)
        second(count - 1)

    loads[3].wait()
    prepare_near(1, p_own, c_own)

    for copy in loads[4:6]:
        copy.wait()
    codes, places, far = lists(near_list_v[...], leaf_links_v[...], first_leaf)
    near_codes_v[...], near_places_v[...], far_codes_v[...] = codes, places, far
    list_copies = []
    for k, (source, target) in enumerate(
        ((near_codes_v, near_codes), (near_places_v, near_places), (far_codes_v, far_codes))
    ):
        copy = pltpu.make_async_copy(source, target, list_sem.at[k])
        copy.start()
        list_copies.append(copy)

    pl.semaphore_wait(barrier, n_narrow + n_wide)
    def gather(count, mine, table, device_of, place, send_sems, recv_sems):
        copies = []
        for step in range(1, count):
            copy = pltpu.make_async_remote_copy(
                src_ref=mine,
                dst_ref=table.at[place],
                send_sem=send_sems.at[step],
                recv_sem=recv_sems.at[step],
                device_id=device_of(step),
                device_id_type=MESH,
            )
            copy.start()
            copies.append(copy)
        table[place] = mine[...]
        return copies

    node_copies = gather(
        n_narrow, node_mine, nodes, lambda step: (g, lax.rem(n + step, n_narrow)), n, node_send, node_recv
    )
    far_halo = send(leaf_skel, s_low, s_high, 2) + send(l_own, l_low, l_high, 3)
    near_halo = send(points, p_low, p_high, 0) + send(charges, c_low, c_high, 1)


    def self_first(i):
        for k in range(NEAR_STEP):
            leaf = i * NEAR_STEP + k
            near_blocks[k] = kernel_block(near_targets[leaf], near_sources[leaves + leaf])

    def self_second(i):
        for k in range(NEAR_STEP):
            leaf = i * NEAR_STEP + k
            sums = dot(near_weights[leaves + leaf], near_blocks[k], NT)
            near[:, pl.ds(pl.multiple_of(leaf * 128, 128), 128)] = sums[:16] + sums[16:]

    stream(leaves // NEAR_STEP, self_first, self_second)

    loads[6].wait()
    prepare_far(1, s_own, l_own)

    for copy in node_copies:
        copy.wait()
    loads[7].wait()
    group = dot(
        twice(jnp.concatenate(in_pairs(nodes, n_narrow), axis=1)), beside(group_upward[...]), NT
    )
    group = group[:16] + group[16:]
    group_mine[...] = jnp.concatenate([group, jnp.zeros_like(group)], axis=1)
    group_copies = gather(
        n_wide, group_mine, groups, lambda step: (lax.rem(g + step, n_wide), n), g, group_send, group_recv
    )

    for copy in list_copies:
        copy.wait()
    for copy in far_halo:
        copy.wait()
    prepare_far(0, s_low, l_low)
    prepare_far(2, s_high, l_high)

    low_s = (lax.rem(lane((48, 256)), 128) < 64).astype(F32).astype(BF16)
    high_s = jnp.ones_like(low_s) - low_s
    low_w, high_w = low_s[:32], high_s[:32]
    far_slots = leaf_links.shape[0]

    def far_picks(i):
        for k in range(FAR_STEP):
            for slot in range(0, far_slots, 2):
                leaf = FAR_STEP * i + k
                yield k, slot // 2, leaf, far_codes[slot, leaf], far_codes[slot + 1, leaf]

    def far_first(i):
        for k, j, leaf, a, b in far_picks(i):
            sources = far_sources[a] * low_s + far_sources[b] * high_s
            far_blocks[k * (far_slots // 2) + j] = kernel_block(far_targets[leaf], sources)

    def far_second(i):
        sums = [jnp.zeros((32, 64), F32)] * FAR_STEP
        for k, j, _, a, b in far_picks(i):
            weights = far_weights[a] * low_w + far_weights[b] * high_w
            sums[k] = sums[k] + dot(weights, far_blocks[k * (far_slots // 2) + j], NT)
        sums = [x[:16] + x[16:] for x in sums]
        for k in range(0, FAR_STEP, 2):
            at = pl.ds(pl.multiple_of((FAR_STEP * i + k) * 64, 128), 128)
            couple_v[:, at] = jnp.concatenate(sums[k : k + 2], axis=1)

    stream(leaves // FAR_STEP, far_first, far_second)
    couple_store = pltpu.make_async_copy(couple_v, couple, load_sem.at[11])
    couple_store.start()

    for copy in near_halo:
        copy.wait()
    prepare_near(0, p_low, c_low)
    prepare_near(2, p_high, c_high)

    def near_code(i, k):
        code = near_codes[0, i * NEAR_STEP + k]
        return code // 1024, lax.rem(code, 1024)

    def near_first(i):
        for k in range(NEAR_STEP):
            t, s = near_code(i, k)
            near_blocks[k] = kernel_block(near_targets[t], near_sources[s])

    def near_second(i):
        for k in range(NEAR_STEP):
            _, s = near_code(i, k)
            sums = dot(near_weights[s], near_blocks[k], NT)
            near_parts[i * NEAR_STEP + k] = sums[:16] + sums[16:]

    stream(NEAR_REST // NEAR_STEP, near_first, near_second)
    near_parts[NEAR_REST] = jnp.zeros((16, 128), F32)

    for copy in group_copies:
        copy.wait()
    for copy in loads[8:11]:
        copy.wait()

    def half_of(skel, start, which):
        tile = source_tile(skel, pl.multiple_of(start, 128), 128)
        at = row((8, 128))
        values = jnp.where(at == 0, tile[0], jnp.where(at == 1, tile[1], tile[2]))
        values = jnp.where(which == 0, values, pltpu.roll(values, 64, 1))
        return values.T[:64]

    def marked(links, base, count):
        at = lane((1, 64 * count)) // 64
        hit = at < 0
        for k in range(links.shape[1]):
            hit = hit | (at == links[0, k] - base)
        return hit.astype(F32)

    def small(target, skel, values, mark):
        kernel = pair_kernel(target, skel) * mark
        sums = dot(twice(jnp.concatenate(values, axis=1)), beside(kernel), NT)
        return sums[:16] + sums[16:]

    group_fields = small(
        half_of(group_skel_v, (g // 2) * 128, lax.rem(g, 2)),
        group_skel_v[...],
        in_pairs(groups, n_wide),
        marked(group_links, 0, n_wide),
    )
    node_fields = dot(group_fields, node_downward_v[...], NN, HIGH) + small(
        half_of(nodes_skel, (n // 2) * 128, lax.rem(n, 2)),
        nodes_skel[...],
        in_pairs(nodes, n_narrow),
        marked(node_links, g * n_narrow, n_narrow),
    )
    fields[...] = node_fields

    def collect(leaf, carry):
        span = pl.ds(pl.multiple_of(leaf * 128, 128), 128)
        value = near[:, span]
        for slot in range(1, near_list.shape[0]):
            value = value + near_parts[near_places[slot, leaf]]
        near[:, span] = value
        return carry

    lax.fori_loop(0, leaves, collect, 0, unroll=8)
    couple_store.wait()


def finish(fields, near, couple, leaf_downward, basis, out):
    field_halves = jnp.concatenate(halves(fields[...]), axis=0)
    low = lane((16, 128)) < 64
    for i in range(basis.shape[0]):
        at = slice(128 * i, 128 * (i + 1))
        product = dot(field_halves, beside(leaf_downward[:, at]), NN)
        leaf = product[:16, :128] + product[16:, :128] + product[:16, 128:] + couple[:, at]
        lefts = [jnp.where(low, leaf, 0.0), jnp.where(low, 0.0, leaf)]
        left = jnp.concatenate([h for x in lefts for h in halves(x)], axis=0)
        product = dot(left, beside(basis[i]), NN)
        for k in range(2):
            rows = product[32 * k : 32 * (k + 1)]
            span = slice(256 * i + 128 * k, 256 * i + 128 * (k + 1))
            out[:, span] = near[:, span] + (rows[:16, :128] + rows[16:, :128] + rows[:16, 128:])


def on_device(
    points,
    charges,
    leaf_skel,
    node_skel,
    group_skel,
    source_basis,
    target_basis,
    leaf_upward,
    leaf_downward,
    node_upward,
    node_downward,
    near_list,
    leaf_links,
    node_links,
    group_links,
):
    n_wide, n_narrow = lax.axis_size("wide"), lax.axis_size("narrow")
    leaves, rank, size = source_basis.shape
    vmem = pl.BlockSpec(memory_space=pltpu.VMEM)
    smem = pl.BlockSpec(memory_space=pltpu.SMEM)
    anywhere = pl.BlockSpec(memory_space=pl.ANY)
    tables = 3 * leaves + 1
    table = (16, 128)
    paired = (leaves // 2, 2 * rank, size)

    def f32(*shape):
        return pltpu.VMEM(shape, F32)

    def bf16(*shape):
        return pltpu.VMEM(shape, BF16)

    def sems(count):
        return pltpu.SemaphoreType.DMA((count,))

    near, couple, fields = pl.pallas_call(
        fused,
        out_shape=[
            jax.ShapeDtypeStruct(charges.shape, F32),
            jax.ShapeDtypeStruct((16, leaf_skel.shape[1]), F32),
            jax.ShapeDtypeStruct((16, rank), F32),
        ],
        in_specs=[anywhere] * 2 + [smem] * 2 + [anywhere] * 9,
        out_specs=[vmem, anywhere, vmem],
        scratch_shapes=[
            *[f32(*points.shape)] * 3,
            *[f32(*charges.shape)] * 3,
            *[f32(*leaf_skel.shape)] * 3,
            *[f32(16, leaf_skel.shape[1])] * 3,
            f32(*paired),
            f32(*leaf_upward.shape),
            f32(64, 64 * n_narrow),
            f32(6, 64 * n_narrow),
            f32(n_narrow, *table),
            f32(n_wide, *table),
            f32(*table),
            f32(*table),
            bf16(tables, 48, 256),
            bf16(tables, 32, 256),
            bf16(leaves, 128, 48),
            bf16(NEAR_STEP, 128, 256),
            f32(NEAR_REST + 1, *table),
            bf16(tables, 48, 256),
            bf16(tables, 32, 256),
            bf16(leaves, 64, 48),
            bf16(4 * FAR_STEP, 64, 256),
            pltpu.VMEM(near_list.shape[::-1], jnp.int32),
            pltpu.VMEM(leaf_links.shape[::-1], jnp.int32),
            f32(*group_skel.shape),
            f32(*node_downward.shape),
            f32(16, leaf_skel.shape[1]),
            pltpu.VMEM((1, 256), jnp.int32),
            pltpu.VMEM((8, 128), jnp.int32),
            pltpu.VMEM((8, 128), jnp.int32),
            pltpu.SMEM((1, 256), jnp.int32),
            pltpu.SMEM((8, 128), jnp.int32),
            pltpu.SMEM((8, 128), jnp.int32),
            sems(12),
            sems(3),
            sems(8),
            sems(8),
            sems(n_narrow),
            sems(n_narrow),
            sems(n_wide),
            sems(n_wide),
        ],
        compiler_params=pltpu.CompilerParams(
            collective_id=0, has_side_effects=True, vmem_limit_bytes=VMEM_LIMIT
        ),
        name="fused",
    )(
        near_list.T,
        leaf_links.T,
        node_links,
        group_links,
        points,
        charges,
        leaf_skel,
        source_basis.reshape(paired),
        leaf_upward,
        node_upward,
        node_skel,
        node_downward,
        group_skel,
    )
    steps = FINISH_STEPS

    def columns(rows, total):
        return pl.BlockSpec((rows, total // steps), lambda i: (0, i))

    return pl.pallas_call(
        finish,
        grid=(steps,),
        out_shape=jax.ShapeDtypeStruct(charges.shape, F32),
        in_specs=[
            pl.BlockSpec(fields.shape, lambda i: (0, 0)),
            columns(*near.shape),
            columns(*couple.shape),
            columns(*leaf_downward.shape),
            pl.BlockSpec((paired[0] // steps, *paired[1:]), lambda i: (i, 0, 0)),
        ],
        out_specs=columns(*near.shape),
        name="finish",
    )(fields, near, couple, leaf_downward, target_basis.reshape(paired))


def solution(mesh):
    both = ("wide", "narrow")
    in_specs = (
        P(None, both),
        P(None, both),
        P(None, both),
        P(),
        P(),
        P(both, None, None),
        P(both, None, None),
        P(None, both),
        P(None, both),
        P(),
        P(None, both),
        P(both, None),
        P(both, None),
        P(both, None),
        P("wide", None),
    )
    return jax.shard_map(
        on_device, mesh=mesh, in_specs=in_specs, out_specs=P(None, both), check_vma=False
    )
```

```python
import math

import jax
import jax.numpy as jnp
from jax import lax
from jax.experimental import pallas as pl
from jax.experimental.pallas import tpu as pltpu
from jax.sharding import PartitionSpec as P

MESH = pl.DeviceIdType.MESH
HIGH = lax.Precision.HIGHEST
F32, BF16 = jnp.float32, jnp.bfloat16
SMOOTH = 0.25
COEFFICIENT = 1.0 / (4.0 * math.pi)
NT = (((1,), (1,)), ((), ()))
NN = (((1,), (0,)), ((), ()))
NEAR_REST = 288 - 64
NEAR_STEP = 32
FAR_STEP = 8
FINISH_STEPS = 4
VMEM_LIMIT = 56 * 2**20


def dot(a, b, dims, precision=None):
    return lax.dot_general(a, b, dims, precision=precision, preferred_element_type=F32)


def halves(x):
    high = x.astype(BF16)
    return high, (x - high.astype(F32)).astype(BF16)


def twice(x):
    high, low = halves(x)
    stacked = jnp.concatenate([high, low], axis=0)
    return jnp.concatenate([stacked, stacked], axis=1)


def beside(x):
    high, low = halves(x)
    return jnp.concatenate([high, low], axis=1)


def pieces(x):
    first = x.astype(BF16).astype(F32)
    rest = x - first
    second = rest.astype(BF16).astype(F32)
    return first, second, rest - second


def lane(shape):
    return lax.broadcasted_iota(jnp.int32, shape, 1)


def row(shape):
    return lax.broadcasted_iota(jnp.int32, shape, 0)


def in_pairs(ref, count):
    return [
        ref[2 * i] + pltpu.roll(ref[2 * i + 1], 64, 1) for i in range(count // 2)
    ]


def source_tile(ref, start, width):
    return [
        jnp.broadcast_to(ref[k : k + 1, pl.ds(start, width)], (8, width)) for k in range(6)
    ]


def source_values(rows):
    y0, y1, y2, m0, m1, m2 = rows
    at = row(y0.shape)
    square = y0 * y0 + y1 * y1 + y2 * y2 + SMOOTH
    flux = (y0 * m0 + y1 * m1 + y2 * m2) * (-COEFFICIENT)
    one, zero = jnp.ones_like(y0), jnp.zeros_like(y0)

    def pick(*terms):
        out = zero
        for k in reversed(range(len(terms))):
            out = jnp.where(at == k, terms[k], out)
        return out

    return (
        pick(-2.0 * y0, -2.0 * y1, -2.0 * y2, square, one),
        pick(COEFFICIENT * m0, COEFFICIENT * m1, COEFFICIENT * m2, flux),
    )


def source_parts(values):
    first, second, third = pieces(values)
    return jnp.concatenate([first, second, third, first, second, first], axis=0).astype(BF16)


def target_parts(rows):
    x0, x1, x2 = rows[:3]
    at = row(x0.shape)
    square = x0 * x0 + x1 * x1 + x2 * x2
    values = jnp.where(at == 0, x0, jnp.where(at == 1, x1, jnp.where(at == 2, x2, 0.0)))
    values = jnp.where(at == 3, 1.0, jnp.where(at == 4, square, values))
    first, second, third = pieces(values)
    fill = jnp.zeros((80, values.shape[1]), F32)
    stacked = jnp.concatenate([first, first, first, second, second, third, fill], axis=0)
    return stacked.T.astype(BF16)[:, :48]


def kernel_block(targets, sources):
    both = dot(targets, sources, NN)
    width = both.shape[1] // 2
    root = lax.rsqrt(both[:, :width])
    return beside((both[:, width:] * root) * (root * root))


def pair_kernel(target, source):
    offset = [target[:, k : k + 1] - source[k : k + 1] for k in range(3)]
    distance = offset[0] * offset[0] + offset[1] * offset[1] + offset[2] * offset[2] + SMOOTH
    flux = offset[0] * source[3:4] + offset[1] * source[4:5] + offset[2] * source[5:6]
    root = lax.rsqrt(distance)
    return (flux * root) * (root * root) * COEFFICIENT


def lists(near, links, first_leaf):
    slots, leaves = near.shape
    fill = jnp.full((slots, 128 - leaves), -1, jnp.int32)
    near = jnp.concatenate([near, fill], axis=1)
    links = jnp.concatenate([links, fill], axis=1)
    spare = 3 * leaves
    far = jnp.where(links < 0, spare, jnp.clip(links - first_leaf, 0, spare - 1))
    across, down = lane(near.shape), row(near.shape)
    used = (near >= 0) & (down > 0)
    count = used.astype(jnp.int32)
    along = count
    step = 1
    while step < leaves:
        along = along + jnp.where(across >= step, pltpu.roll(along, step, 1), 0)
        step *= 2
    totals = jnp.broadcast_to(along[:, leaves - 1 : leaves], along.shape)
    above = totals
    step = 1
    while step < slots:
        above = above + jnp.where(down >= step, pltpu.roll(above, step, 0), 0)
        step *= 2
    place = along - count + above - totals
    place = jnp.where(used, jnp.minimum(place, NEAR_REST), NEAR_REST)
    code = across * 1024 + jnp.clip(near - first_leaf, 0, spare - 1) + 1
    places, codes = place.T[:leaves], code.T[:leaves]
    at = lane((leaves, 256))
    hits = jnp.zeros((leaves, 256), jnp.int32)
    for slot in range(1, slots):
        hits = hits + jnp.where(places[:, slot : slot + 1] == at, codes[:, slot : slot + 1], 0)
    packed = jnp.sum(hits, axis=0, keepdims=True)
    return jnp.where((packed > 0) & (lane((1, 256)) < NEAR_REST), packed - 1, spare), place, far


def fused(
    near_list,
    leaf_links,
    node_links,
    group_links,
    points,
    charges,
    leaf_skel,
    source_basis,
    leaf_upward,
    node_upward,
    node_skel,
    node_downward,
    group_skel,
    near,
    couple,
    fields,
    p_low,
    p_own,
    p_high,
    c_low,
    c_own,
    c_high,
    s_low,
    s_own,
    s_high,
    l_low,
    l_own,
    l_high,
    basis_up,
    upward_own,
    group_upward,
    nodes_skel,
    nodes,
    groups,
    node_mine,
    group_mine,
    near_sources,
    near_weights,
    near_targets,
    near_blocks,
    near_parts,
    far_sources,
    far_weights,
    far_targets,
    far_blocks,
    near_list_v,
    leaf_links_v,
    group_skel_v,
    node_downward_v,
    couple_v,
    near_codes_v,
    near_places_v,
    far_codes_v,
    near_codes,
    near_places,
    far_codes,
    load_sem,
    list_sem,
    halo_send,
    halo_recv,
    node_send,
    node_recv,
    group_send,
    group_recv,
):
    n_wide, n_narrow = lax.axis_size("wide"), lax.axis_size("narrow")
    g, n = lax.axis_index("wide"), lax.axis_index("narrow")
    leaves = leaf_links.shape[1]
    spare = 3 * leaves
    first_leaf = (g * n_narrow + n) * leaves - leaves
    at_end = (n == n_narrow - 1).astype(jnp.int32)
    at_start = (n == 0).astype(jnp.int32)
    after = (lax.rem(g + at_end, n_wide), lax.rem(n + 1, n_narrow))
    before = (
        lax.rem(g - at_start + n_wide, n_wide),
        lax.rem(n - 1 + n_narrow, n_narrow),
    )
    group_span = pl.ds(pl.multiple_of(g * (64 * n_narrow), 128), 64 * n_narrow)

    loads = []
    for k, (source, target) in enumerate(
        (
            (charges, c_own),
            (source_basis, basis_up),
            (leaf_upward, upward_own),
            (points, p_own),
            (near_list, near_list_v),
            (leaf_links, leaf_links_v),
            (leaf_skel, s_own),
            (node_upward.at[:, group_span], group_upward),
            (node_skel.at[:, group_span], nodes_skel),
            (group_skel, group_skel_v),
            (node_downward, node_downward_v),
        )
    ):
        copy = pltpu.make_async_copy(source, target, load_sem.at[k])
        copy.start()
        loads.append(copy)

    barrier = pltpu.get_barrier_semaphore()
    for device in (after, before):
        pl.semaphore_signal(barrier, inc=1, device_id=device, device_id_type=MESH)
    for step in range(1, n_narrow):
        pl.semaphore_signal(
            barrier, inc=1, device_id=(g, lax.rem(n + step, n_narrow)), device_id_type=MESH
        )
    for step in range(1, n_wide):
        pl.semaphore_signal(
            barrier, inc=1, device_id=(lax.rem(g + step, n_wide), n), device_id_type=MESH
        )

    pl.semaphore_wait(barrier, n_narrow + n_wide)

    def send(source, low, high, at):
        copies = []
        for target, device, k in ((low, after, 2 * at), (high, before, 2 * at + 1)):
            copy = pltpu.make_async_remote_copy(
                src_ref=source,
                dst_ref=target,
                send_sem=halo_send.at[k],
                recv_sem=halo_recv.at[k],
                device_id=device,
                device_id_type=MESH,
            )
            copy.start()
            copies.append(copy)
        return copies

    far_halo = send(leaf_skel, s_low, s_high, 2)
    near_halo = send(points, p_low, p_high, 0)

    for copy in loads[:3]:
        copy.wait()

    def upward(i, total):
        first = c_own[:, pl.ds(pl.multiple_of(i * 256, 256), 128)]
        second = c_own[:, pl.ds(pl.multiple_of(i * 256 + 128, 128), 128)]
        weights = jnp.concatenate([twice(first), twice(second)], axis=0)
        product = dot(weights, beside(basis_up[i]), NT)
        values = jnp.where(
            lane((16, 128)) < 64,
            product[0:16] + product[16:32],
            product[32:48] + product[48:64],
        )
        at = pl.ds(pl.multiple_of(i * 128, 128), 128)
        l_own[:, at] = values
        return total + dot(twice(values), beside(upward_own[:, at]), NT)

    total = lax.fori_loop(0, leaves // 2, upward, jnp.zeros((32, 64), F32), unroll=16)
    own = total[:16] + total[16:]
    node_mine[...] = jnp.concatenate([own, jnp.zeros_like(own)], axis=1)

    def gather(count, mine, table, device_of, place, send_sems, recv_sems):
        copies = []
        for step in range(1, count):
            copy = pltpu.make_async_remote_copy(
                src_ref=mine,
                dst_ref=table.at[place],
                send_sem=send_sems.at[step],
                recv_sem=recv_sems.at[step],
                device_id=device_of(step),
                device_id_type=MESH,
            )
            copy.start()
            copies.append(copy)
        table[place] = mine[...]
        return copies

    node_copies = gather(
        n_narrow, node_mine, nodes, lambda step: (g, lax.rem(n + step, n_narrow)), n, node_send, node_recv
    )
    far_halo += send(l_own, l_low, l_high, 3)

    zero_rows = [jnp.zeros((8, 128), F32)] * 6
    for table in (near_sources, far_sources):
        parts = [source_parts(v) for v in source_values(zero_rows)]
        table[spare] = jnp.concatenate(parts, axis=1)
    for table in (near_weights, far_weights):
        table[spare] = jnp.zeros(table.shape[1:], BF16)

    def prepare_near(side, points_ref, charges_ref):
        def body(i, carry):
            start = pl.multiple_of(i * 128, 128)
            rows = source_tile(points_ref, start, 128)
            parts = [source_parts(v) for v in source_values(rows)]
            near_sources[side * leaves + i] = jnp.concatenate(parts, axis=1)
            near_weights[side * leaves + i] = twice(charges_ref[:, pl.ds(start, 128)])
            if side == 1:
                near_targets[i] = target_parts(rows)
            return carry

        lax.fori_loop(0, leaves, body, 0, unroll=8)

    def both_halves(x):
        low = lane(x.shape) < 64
        turned = pltpu.roll(x, 64, 1)
        return jnp.where(low, x, turned), jnp.where(low, turned, x)

    def prepare_far(side, points_ref, charges_ref):
        def body(i, carry):
            start = pl.multiple_of(i * 128, 128)
            rows = source_tile(points_ref, start, 128)
            split = [both_halves(v) for v in source_values(rows)]
            weights = both_halves(charges_ref[:, pl.ds(start, 128)])
            for k in range(2):
                parts = [source_parts(v[k]) for v in split]
                far_sources[side * leaves + 2 * i + k] = jnp.concatenate(parts, axis=1)
                far_weights[side * leaves + 2 * i + k] = twice(weights[k])
            if side == 1:
                targets = target_parts(rows)
                far_targets[2 * i] = targets[:64]
                far_targets[2 * i + 1] = targets[64:]
            return carry

        lax.fori_loop(0, leaves // 2, body, 0, unroll=8)

    def stream(count, first, second):
        first(0)

        def body(i, carry):
            second(i - 1)
            first(i)
            return carry

        lax.fori_loop(1, count, body, 0)
        second(count - 1)

    loads[3].wait()
    prepare_near(1, p_own, c_own)
    near_halo += send(charges, c_low, c_high, 1)

    for copy in loads[4:6]:
        copy.wait()
    codes, places, far = lists(near_list_v[...], leaf_links_v[...], first_leaf)
    near_codes_v[...], near_places_v[...], far_codes_v[...] = codes, places, far
    list_copies = []
    for k, (source, target) in enumerate(
        ((near_codes_v, near_codes), (near_places_v, near_places), (far_codes_v, far_codes))
    ):
        copy = pltpu.make_async_copy(source, target, list_sem.at[k])
        copy.start()
        list_copies.append(copy)

    def self_first(i):
        for k in range(NEAR_STEP):
            leaf = i * NEAR_STEP + k
            near_blocks[k] = kernel_block(near_targets[leaf], near_sources[leaves + leaf])

    def self_second(i):
        for k in range(NEAR_STEP):
            leaf = i * NEAR_STEP + k
            sums = dot(near_weights[leaves + leaf], near_blocks[k], NT)
            near[:, pl.ds(pl.multiple_of(leaf * 128, 128), 128)] = sums[:16] + sums[16:]

    stream(leaves // NEAR_STEP, self_first, self_second)

    loads[6].wait()
    prepare_far(1, s_own, l_own)

    for copy in node_copies:
        copy.wait()
    loads[7].wait()
    group = dot(
        twice(jnp.concatenate(in_pairs(nodes, n_narrow), axis=1)), beside(group_upward[...]), NT
    )
    group = group[:16] + group[16:]
    group_mine[...] = jnp.concatenate([group, jnp.zeros_like(group)], axis=1)
    group_copies = gather(
        n_wide, group_mine, groups, lambda step: (lax.rem(g + step, n_wide), n), g, group_send, group_recv
    )

    for copy in list_copies:
        copy.wait()
    for copy in far_halo:
        copy.wait()
    prepare_far(0, s_low, l_low)
    prepare_far(2, s_high, l_high)

    low_s = (lax.rem(lane((48, 256)), 128) < 64).astype(F32).astype(BF16)
    high_s = jnp.ones_like(low_s) - low_s
    low_w, high_w = low_s[:32], high_s[:32]
    far_slots = leaf_links.shape[0]

    def far_picks(i):
        for k in range(FAR_STEP):
            for slot in range(0, far_slots, 2):
                leaf = FAR_STEP * i + k
                yield k, slot // 2, leaf, far_codes[slot, leaf], far_codes[slot + 1, leaf]

    def far_first(i):
        for k, j, leaf, a, b in far_picks(i):
            sources = far_sources[a] * low_s + far_sources[b] * high_s
            far_blocks[k * (far_slots // 2) + j] = kernel_block(far_targets[leaf], sources)

    def far_second(i):
        sums = [jnp.zeros((32, 64), F32)] * FAR_STEP
        for k, j, _, a, b in far_picks(i):
            weights = far_weights[a] * low_w + far_weights[b] * high_w
            sums[k] = sums[k] + dot(weights, far_blocks[k * (far_slots // 2) + j], NT)
        sums = [x[:16] + x[16:] for x in sums]
        for k in range(0, FAR_STEP, 2):
            at = pl.ds(pl.multiple_of((FAR_STEP * i + k) * 64, 128), 128)
            couple_v[:, at] = jnp.concatenate(sums[k : k + 2], axis=1)

    stream(leaves // FAR_STEP, far_first, far_second)
    couple_store = pltpu.make_async_copy(couple_v, couple, load_sem.at[11])
    couple_store.start()

    for copy in near_halo:
        copy.wait()
    prepare_near(0, p_low, c_low)
    prepare_near(2, p_high, c_high)

    def near_code(i, k):
        code = near_codes[0, i * NEAR_STEP + k]
        return code // 1024, lax.rem(code, 1024)

    def near_first(i):
        for k in range(NEAR_STEP):
            t, s = near_code(i, k)
            near_blocks[k] = kernel_block(near_targets[t], near_sources[s])

    def near_second(i):
        for k in range(NEAR_STEP):
            _, s = near_code(i, k)
            sums = dot(near_weights[s], near_blocks[k], NT)
            near_parts[i * NEAR_STEP + k] = sums[:16] + sums[16:]

    stream(NEAR_REST // NEAR_STEP, near_first, near_second)
    near_parts[NEAR_REST] = jnp.zeros((16, 128), F32)

    for copy in group_copies:
        copy.wait()
    for copy in loads[8:11]:
        copy.wait()

    def half_of(skel, start, which):
        tile = source_tile(skel, pl.multiple_of(start, 128), 128)
        at = row((8, 128))
        values = jnp.where(at == 0, tile[0], jnp.where(at == 1, tile[1], tile[2]))
        values = jnp.where(which == 0, values, pltpu.roll(values, 64, 1))
        return values.T[:64]

    def marked(links, base, count):
        at = lane((1, 64 * count)) // 64
        hit = at < 0
        for k in range(links.shape[1]):
            hit = hit | (at == links[0, k] - base)
        return hit.astype(F32)

    def small(target, skel, values, mark):
        kernel = pair_kernel(target, skel) * mark
        sums = dot(twice(jnp.concatenate(values, axis=1)), beside(kernel), NT)
        return sums[:16] + sums[16:]

    group_fields = small(
        half_of(group_skel_v, (g // 2) * 128, lax.rem(g, 2)),
        group_skel_v[...],
        in_pairs(groups, n_wide),
        marked(group_links, 0, n_wide),
    )
    node_fields = dot(group_fields, node_downward_v[...], NN, HIGH) + small(
        half_of(nodes_skel, (n // 2) * 128, lax.rem(n, 2)),
        nodes_skel[...],
        in_pairs(nodes, n_narrow),
        marked(node_links, g * n_narrow, n_narrow),
    )
    fields[...] = node_fields

    def collect(leaf, carry):
        span = pl.ds(pl.multiple_of(leaf * 128, 128), 128)
        value = near[:, span]
        for slot in range(1, near_list.shape[0]):
            value = value + near_parts[near_places[slot, leaf]]
        near[:, span] = value
        return carry

    lax.fori_loop(0, leaves, collect, 0, unroll=8)
    couple_store.wait()


def finish(fields, near, couple, leaf_downward, basis, out):
    field_halves = jnp.concatenate(halves(fields[...]), axis=0)
    low = lane((16, 128)) < 64
    for i in range(basis.shape[0]):
        at = slice(128 * i, 128 * (i + 1))
        product = dot(field_halves, beside(leaf_downward[:, at]), NN)
        leaf = product[:16, :128] + product[16:, :128] + product[:16, 128:] + couple[:, at]
        lefts = [jnp.where(low, leaf, 0.0), jnp.where(low, 0.0, leaf)]
        left = jnp.concatenate([h for x in lefts for h in halves(x)], axis=0)
        product = dot(left, beside(basis[i]), NN)
        for k in range(2):
            rows = product[32 * k : 32 * (k + 1)]
            span = slice(256 * i + 128 * k, 256 * i + 128 * (k + 1))
            out[:, span] = near[:, span] + (rows[:16, :128] + rows[16:, :128] + rows[:16, 128:])


def on_device(
    points,
    charges,
    leaf_skel,
    node_skel,
    group_skel,
    source_basis,
    target_basis,
    leaf_upward,
    leaf_downward,
    node_upward,
    node_downward,
    near_list,
    leaf_links,
    node_links,
    group_links,
):
    n_wide, n_narrow = lax.axis_size("wide"), lax.axis_size("narrow")
    leaves, rank, size = source_basis.shape
    vmem = pl.BlockSpec(memory_space=pltpu.VMEM)
    smem = pl.BlockSpec(memory_space=pltpu.SMEM)
    anywhere = pl.BlockSpec(memory_space=pl.ANY)
    tables = 3 * leaves + 1
    table = (16, 128)
    paired = (leaves // 2, 2 * rank, size)

    def f32(*shape):
        return pltpu.VMEM(shape, F32)

    def bf16(*shape):
        return pltpu.VMEM(shape, BF16)

    def sems(count):
        return pltpu.SemaphoreType.DMA((count,))

    near, couple, fields = pl.pallas_call(
        fused,
        out_shape=[
            jax.ShapeDtypeStruct(charges.shape, F32),
            jax.ShapeDtypeStruct((16, leaf_skel.shape[1]), F32),
            jax.ShapeDtypeStruct((16, rank), F32),
        ],
        in_specs=[anywhere] * 2 + [smem] * 2 + [anywhere] * 9,
        out_specs=[vmem, anywhere, vmem],
        scratch_shapes=[
            *[f32(*points.shape)] * 3,
            *[f32(*charges.shape)] * 3,
            *[f32(*leaf_skel.shape)] * 3,
            *[f32(16, leaf_skel.shape[1])] * 3,
            f32(*paired),
            f32(*leaf_upward.shape),
            f32(64, 64 * n_narrow),
            f32(6, 64 * n_narrow),
            f32(n_narrow, *table),
            f32(n_wide, *table),
            f32(*table),
            f32(*table),
            bf16(tables, 48, 256),
            bf16(tables, 32, 256),
            bf16(leaves, 128, 48),
            bf16(NEAR_STEP, 128, 256),
            f32(NEAR_REST + 1, *table),
            bf16(tables, 48, 256),
            bf16(tables, 32, 256),
            bf16(leaves, 64, 48),
            bf16(4 * FAR_STEP, 64, 256),
            pltpu.VMEM(near_list.shape[::-1], jnp.int32),
            pltpu.VMEM(leaf_links.shape[::-1], jnp.int32),
            f32(*group_skel.shape),
            f32(*node_downward.shape),
            f32(16, leaf_skel.shape[1]),
            pltpu.VMEM((1, 256), jnp.int32),
            pltpu.VMEM((8, 128), jnp.int32),
            pltpu.VMEM((8, 128), jnp.int32),
            pltpu.SMEM((1, 256), jnp.int32),
            pltpu.SMEM((8, 128), jnp.int32),
            pltpu.SMEM((8, 128), jnp.int32),
            sems(12),
            sems(3),
            sems(8),
            sems(8),
            sems(n_narrow),
            sems(n_narrow),
            sems(n_wide),
            sems(n_wide),
        ],
        compiler_params=pltpu.CompilerParams(
            collective_id=0, has_side_effects=True, vmem_limit_bytes=VMEM_LIMIT
        ),
        name="fused",
    )(
        near_list.T,
        leaf_links.T,
        node_links,
        group_links,
        points,
        charges,
        leaf_skel,
        source_basis.reshape(paired),
        leaf_upward,
        node_upward,
        node_skel,
        node_downward,
        group_skel,
    )
    steps = FINISH_STEPS

    def columns(rows, total):
        return pl.BlockSpec((rows, total // steps), lambda i: (0, i))

    return pl.pallas_call(
        finish,
        grid=(steps,),
        out_shape=jax.ShapeDtypeStruct(charges.shape, F32),
        in_specs=[
            pl.BlockSpec(fields.shape, lambda i: (0, 0)),
            columns(*near.shape),
            columns(*couple.shape),
            columns(*leaf_downward.shape),
            pl.BlockSpec((paired[0] // steps, *paired[1:]), lambda i: (i, 0, 0)),
        ],
        out_specs=columns(*near.shape),
        name="finish",
    )(fields, near, couple, leaf_downward, target_basis.reshape(paired))


def solution(mesh):
    both = ("wide", "narrow")
    in_specs = (
        P(None, both),
        P(None, both),
        P(None, both),
        P(),
        P(),
        P(both, None, None),
        P(both, None, None),
        P(None, both),
        P(None, both),
        P(),
        P(None, both),
        P(both, None),
        P(both, None),
        P(both, None),
        P("wide", None),
    )
    return jax.shard_map(
        on_device, mesh=mesh, in_specs=in_specs, out_specs=P(None, both), check_vma=False
    )
```

```python
import math

import jax
import jax.numpy as jnp
from jax import lax
from jax.experimental import pallas as pl
from jax.experimental.pallas import tpu as pltpu
from jax.sharding import PartitionSpec as P

MESH = pl.DeviceIdType.MESH
HIGH = lax.Precision.HIGHEST
F32, BF16 = jnp.float32, jnp.bfloat16
SMOOTH = 0.25
COEFFICIENT = 1.0 / (4.0 * math.pi)
NT = (((1,), (1,)), ((), ()))
NN = (((1,), (0,)), ((), ()))
NEAR_REST = 288 - 64
NEAR_STEP = 32
REST_STEP = 56
FAR_STEP = 16
FINISH_STEPS = 4
VMEM_LIMIT = 56 * 2**20


def dot(a, b, dims, precision=None):
    return lax.dot_general(a, b, dims, precision=precision, preferred_element_type=F32)


def halves(x):
    high = x.astype(BF16)
    return high, (x - high.astype(F32)).astype(BF16)


def twice(x):
    high, low = halves(x)
    stacked = jnp.concatenate([high, low], axis=0)
    return jnp.concatenate([stacked, stacked], axis=1)


def beside(x):
    high, low = halves(x)
    return jnp.concatenate([high, low], axis=1)


def pieces(x):
    first = x.astype(BF16).astype(F32)
    rest = x - first
    second = rest.astype(BF16).astype(F32)
    return first, second, rest - second


def lane(shape):
    return lax.broadcasted_iota(jnp.int32, shape, 1)


def row(shape):
    return lax.broadcasted_iota(jnp.int32, shape, 0)


def in_pairs(ref, count):
    return [
        ref[2 * i] + pltpu.roll(ref[2 * i + 1], 64, 1) for i in range(count // 2)
    ]


def source_tile(ref, start, width):
    return [
        jnp.broadcast_to(ref[k : k + 1, pl.ds(start, width)], (8, width)) for k in range(6)
    ]


def source_values(rows):
    y0, y1, y2, m0, m1, m2 = rows
    at = row(y0.shape)
    square = y0 * y0 + y1 * y1 + y2 * y2 + SMOOTH
    flux = (y0 * m0 + y1 * m1 + y2 * m2) * (-COEFFICIENT)
    one, zero = jnp.ones_like(y0), jnp.zeros_like(y0)

    def pick(*terms):
        out = zero
        for k in reversed(range(len(terms))):
            out = jnp.where(at == k, terms[k], out)
        return out

    return (
        pick(-2.0 * y0, -2.0 * y1, -2.0 * y2, square, one),
        pick(COEFFICIENT * m0, COEFFICIENT * m1, COEFFICIENT * m2, flux),
    )


def source_parts(values):
    first, second, third = pieces(values)
    return jnp.concatenate([first, second, third, first, second, first], axis=0).astype(BF16)


def target_parts(rows):
    x0, x1, x2 = rows[:3]
    at = row(x0.shape)
    square = x0 * x0 + x1 * x1 + x2 * x2
    values = jnp.where(at == 0, x0, jnp.where(at == 1, x1, jnp.where(at == 2, x2, 0.0)))
    values = jnp.where(at == 3, 1.0, jnp.where(at == 4, square, values))
    first, second, third = pieces(values)
    fill = jnp.zeros((80, values.shape[1]), F32)
    stacked = jnp.concatenate([first, first, first, second, second, third, fill], axis=0)
    return stacked.T.astype(BF16)[:, :48]


def kernel_block(targets, sources):
    both = dot(targets, sources, NN)
    width = both.shape[1] // 2
    root = lax.rsqrt(both[:, :width])
    return beside((both[:, width:] * root) * (root * root))


def pair_kernel(target, source):
    offset = [target[:, k : k + 1] - source[k : k + 1] for k in range(3)]
    distance = offset[0] * offset[0] + offset[1] * offset[1] + offset[2] * offset[2] + SMOOTH
    flux = offset[0] * source[3:4] + offset[1] * source[4:5] + offset[2] * source[5:6]
    root = lax.rsqrt(distance)
    return (flux * root) * (root * root) * COEFFICIENT


def lists(near, links, first_leaf):
    slots, leaves = near.shape
    fill = jnp.full((slots, 128 - leaves), -1, jnp.int32)
    near = jnp.concatenate([near, fill], axis=1)
    links = jnp.concatenate([links, fill], axis=1)
    spare = 3 * leaves
    far = jnp.where(links < 0, spare, jnp.clip(links - first_leaf, 0, spare - 1))
    across, down = lane(near.shape), row(near.shape)
    used = (near >= 0) & (down > 0)
    count = used.astype(jnp.int32)
    along = count
    step = 1
    while step < leaves:
        along = along + jnp.where(across >= step, pltpu.roll(along, step, 1), 0)
        step *= 2
    totals = jnp.broadcast_to(along[:, leaves - 1 : leaves], along.shape)
    above = totals
    step = 1
    while step < slots:
        above = above + jnp.where(down >= step, pltpu.roll(above, step, 0), 0)
        step *= 2
    place = along - count + above - totals
    place = jnp.where(used, jnp.minimum(place, NEAR_REST), NEAR_REST)
    code = across * 1024 + jnp.clip(near - first_leaf, 0, spare - 1) + 1
    places, codes = place.T[:leaves], code.T[:leaves]
    at = lane((leaves, 256))
    hits = jnp.zeros((leaves, 256), jnp.int32)
    for slot in range(1, slots):
        hits = hits + jnp.where(places[:, slot : slot + 1] == at, codes[:, slot : slot + 1], 0)
    packed = jnp.sum(hits, axis=0, keepdims=True)
    return jnp.where((packed > 0) & (lane((1, 256)) < NEAR_REST), packed - 1, spare), place, far


def fused(
    near_list,
    leaf_links,
    node_links,
    group_links,
    points,
    charges,
    leaf_skel,
    source_basis,
    leaf_upward,
    node_upward,
    node_skel,
    node_downward,
    group_skel,
    near,
    couple,
    fields,
    p_low,
    p_own,
    p_high,
    c_low,
    c_own,
    c_high,
    s_low,
    s_own,
    s_high,
    l_low,
    l_own,
    l_high,
    basis_up,
    upward_own,
    group_upward,
    nodes_skel,
    nodes,
    groups,
    node_mine,
    group_mine,
    near_sources,
    near_weights,
    near_targets,
    near_blocks,
    near_parts,
    far_sources,
    far_weights,
    far_targets,
    far_blocks,
    near_list_v,
    leaf_links_v,
    group_skel_v,
    node_downward_v,
    couple_v,
    near_codes_v,
    near_places_v,
    far_codes_v,
    near_codes,
    near_places,
    far_codes,
    load_sem,
    list_sem,
    halo_send,
    halo_recv,
    node_send,
    node_recv,
    group_send,
    group_recv,
):
    n_wide, n_narrow = lax.axis_size("wide"), lax.axis_size("narrow")
    g, n = lax.axis_index("wide"), lax.axis_index("narrow")
    leaves = leaf_links.shape[1]
    spare = 3 * leaves
    first_leaf = (g * n_narrow + n) * leaves - leaves
    at_end = (n == n_narrow - 1).astype(jnp.int32)
    at_start = (n == 0).astype(jnp.int32)
    after = (lax.rem(g + at_end, n_wide), lax.rem(n + 1, n_narrow))
    before = (
        lax.rem(g - at_start + n_wide, n_wide),
        lax.rem(n - 1 + n_narrow, n_narrow),
    )
    group_span = pl.ds(pl.multiple_of(g * (64 * n_narrow), 128), 64 * n_narrow)

    loads = []
    for k, (source, target) in enumerate(
        (
            (charges, c_own),
            (source_basis, basis_up),
            (leaf_upward, upward_own),
            (points, p_own),
            (near_list, near_list_v),
            (leaf_links, leaf_links_v),
            (leaf_skel, s_own),
            (node_upward.at[:, group_span], group_upward),
            (node_skel.at[:, group_span], nodes_skel),
            (group_skel, group_skel_v),
            (node_downward, node_downward_v),
        )
    ):
        copy = pltpu.make_async_copy(source, target, load_sem.at[k])
        copy.start()
        loads.append(copy)

    barrier = pltpu.get_barrier_semaphore()
    for device in (after, before):
        pl.semaphore_signal(barrier, inc=1, device_id=device, device_id_type=MESH)
    for step in range(1, n_narrow):
        pl.semaphore_signal(
            barrier, inc=1, device_id=(g, lax.rem(n + step, n_narrow)), device_id_type=MESH
        )
    for step in range(1, n_wide):
        pl.semaphore_signal(
            barrier, inc=1, device_id=(lax.rem(g + step, n_wide), n), device_id_type=MESH
        )

    pl.semaphore_wait(barrier, n_narrow + n_wide)

    def send(source, low, high, at):
        copies = []
        for target, device, k in ((low, after, 2 * at), (high, before, 2 * at + 1)):
            copy = pltpu.make_async_remote_copy(
                src_ref=source,
                dst_ref=target,
                send_sem=halo_send.at[k],
                recv_sem=halo_recv.at[k],
                device_id=device,
                device_id_type=MESH,
            )
            copy.start()
            copies.append(copy)
        return copies

    far_halo = send(leaf_skel, s_low, s_high, 2)
    near_halo = send(points, p_low, p_high, 0)

    for copy in loads[:3]:
        copy.wait()

    def upward(i, total):
        first = c_own[:, pl.ds(pl.multiple_of(i * 256, 256), 128)]
        second = c_own[:, pl.ds(pl.multiple_of(i * 256 + 128, 128), 128)]
        weights = jnp.concatenate([twice(first), twice(second)], axis=0)
        product = dot(weights, beside(basis_up[i]), NT)
        values = jnp.where(
            lane((16, 128)) < 64,
            product[0:16] + product[16:32],
            product[32:48] + product[48:64],
        )
        at = pl.ds(pl.multiple_of(i * 128, 128), 128)
        l_own[:, at] = values
        return total + dot(twice(values), beside(upward_own[:, at]), NT)

    total = lax.fori_loop(0, leaves // 2, upward, jnp.zeros((32, 64), F32), unroll=16)
    own = total[:16] + total[16:]
    node_mine[...] = jnp.concatenate([own, jnp.zeros_like(own)], axis=1)

    def gather(count, mine, table, device_of, place, send_sems, recv_sems):
        copies = []
        for step in range(1, count):
            copy = pltpu.make_async_remote_copy(
                src_ref=mine,
                dst_ref=table.at[place],
                send_sem=send_sems.at[step],
                recv_sem=recv_sems.at[step],
                device_id=device_of(step),
                device_id_type=MESH,
            )
            copy.start()
            copies.append(copy)
        table[place] = mine[...]
        return copies

    node_copies = gather(
        n_narrow, node_mine, nodes, lambda step: (g, lax.rem(n + step, n_narrow)), n, node_send, node_recv
    )
    far_halo += send(l_own, l_low, l_high, 3)

    zero_rows = [jnp.zeros((8, 128), F32)] * 6
    for table in (near_sources, far_sources):
        parts = [source_parts(v) for v in source_values(zero_rows)]
        table[spare] = jnp.concatenate(parts, axis=1)
    for table in (near_weights, far_weights):
        table[spare] = jnp.zeros(table.shape[1:], BF16)

    def prepare_near(side, points_ref, charges_ref):
        def body(i, carry):
            start = pl.multiple_of(i * 128, 128)
            rows = source_tile(points_ref, start, 128)
            parts = [source_parts(v) for v in source_values(rows)]
            near_sources[side * leaves + i] = jnp.concatenate(parts, axis=1)
            near_weights[side * leaves + i] = twice(charges_ref[:, pl.ds(start, 128)])
            if side == 1:
                near_targets[i] = target_parts(rows)
            return carry

        lax.fori_loop(0, leaves, body, 0, unroll=8)

    def both_halves(x):
        low = lane(x.shape) < 64
        turned = pltpu.roll(x, 64, 1)
        return jnp.where(low, x, turned), jnp.where(low, turned, x)

    def prepare_far(side, points_ref, charges_ref):
        def body(i, carry):
            start = pl.multiple_of(i * 128, 128)
            rows = source_tile(points_ref, start, 128)
            split = [both_halves(v) for v in source_values(rows)]
            weights = both_halves(charges_ref[:, pl.ds(start, 128)])
            for k in range(2):
                parts = [source_parts(v[k]) for v in split]
                far_sources[side * leaves + 2 * i + k] = jnp.concatenate(parts, axis=1)
                far_weights[side * leaves + 2 * i + k] = twice(weights[k])
            if side == 1:
                targets = target_parts(rows)
                far_targets[2 * i] = targets[:64]
                far_targets[2 * i + 1] = targets[64:]
            return carry

        lax.fori_loop(0, leaves // 2, body, 0, unroll=8)

    def stream(count, first, second):
        first(0)

        def body(i, carry):
            second(i - 1)
            first(i)
            return carry

        lax.fori_loop(1, count, body, 0)
        second(count - 1)

    loads[3].wait()
    prepare_near(1, p_own, c_own)
    near_halo += send(charges, c_low, c_high, 1)

    for copy in loads[4:6]:
        copy.wait()
    codes, places, far = lists(near_list_v[...], leaf_links_v[...], first_leaf)
    near_codes_v[...], near_places_v[...], far_codes_v[...] = codes, places, far
    list_copies = []
    for k, (source, target) in enumerate(
        ((near_codes_v, near_codes), (near_places_v, near_places), (far_codes_v, far_codes))
    ):
        copy = pltpu.make_async_copy(source, target, list_sem.at[k])
        copy.start()
        list_copies.append(copy)

    def self_first(i):
        for k in range(NEAR_STEP):
            leaf = i * NEAR_STEP + k
            near_blocks[k] = kernel_block(near_targets[leaf], near_sources[leaves + leaf])

    def self_second(i):
        for k in range(NEAR_STEP):
            leaf = i * NEAR_STEP + k
            sums = dot(near_weights[leaves + leaf], near_blocks[k], NT)
            near[:, pl.ds(pl.multiple_of(leaf * 128, 128), 128)] = sums[:16] + sums[16:]

    stream(leaves // NEAR_STEP, self_first, self_second)

    loads[6].wait()
    prepare_far(1, s_own, l_own)

    for copy in node_copies:
        copy.wait()
    loads[7].wait()
    group = dot(
        twice(jnp.concatenate(in_pairs(nodes, n_narrow), axis=1)), beside(group_upward[...]), NT
    )
    group = group[:16] + group[16:]
    group_mine[...] = jnp.concatenate([group, jnp.zeros_like(group)], axis=1)
    group_copies = gather(
        n_wide, group_mine, groups, lambda step: (lax.rem(g + step, n_wide), n), g, group_send, group_recv
    )

    for copy in list_copies:
        copy.wait()
    for copy in far_halo:
        copy.wait()
    prepare_far(0, s_low, l_low)
    prepare_far(2, s_high, l_high)

    low_s = (lax.rem(lane((48, 256)), 128) < 64).astype(F32).astype(BF16)
    high_s = jnp.ones_like(low_s) - low_s
    low_w, high_w = low_s[:32], high_s[:32]
    far_slots = leaf_links.shape[0]

    def far_picks(i):
        for k in range(FAR_STEP):
            for slot in range(0, far_slots, 2):
                leaf = FAR_STEP * i + k
                yield k, slot // 2, leaf, far_codes[slot, leaf], far_codes[slot + 1, leaf]

    def far_first(i):
        for k, j, leaf, a, b in far_picks(i):
            sources = far_sources[a] * low_s + far_sources[b] * high_s
            far_blocks[k * (far_slots // 2) + j] = kernel_block(far_targets[leaf], sources)

    def far_second(i):
        sums = [jnp.zeros((32, 64), F32)] * FAR_STEP
        for k, j, _, a, b in far_picks(i):
            weights = far_weights[a] * low_w + far_weights[b] * high_w
            sums[k] = sums[k] + dot(weights, far_blocks[k * (far_slots // 2) + j], NT)
        sums = [x[:16] + x[16:] for x in sums]
        for k in range(0, FAR_STEP, 2):
            at = pl.ds(pl.multiple_of((FAR_STEP * i + k) * 64, 128), 128)
            couple_v[:, at] = jnp.concatenate(sums[k : k + 2], axis=1)

    stream(leaves // FAR_STEP, far_first, far_second)
    couple_store = pltpu.make_async_copy(couple_v, couple, load_sem.at[11])
    couple_store.start()

    for copy in near_halo:
        copy.wait()
    prepare_near(0, p_low, c_low)
    prepare_near(2, p_high, c_high)

    def near_code(i, k):
        code = near_codes[0, i * REST_STEP + k]
        return code // 1024, lax.rem(code, 1024)

    def near_first(i):
        for k in range(REST_STEP):
            t, s = near_code(i, k)
            near_blocks[k] = kernel_block(near_targets[t], near_sources[s])

    def near_second(i):
        for k in range(REST_STEP):
            _, s = near_code(i, k)
            sums = dot(near_weights[s], near_blocks[k], NT)
            near_parts[i * REST_STEP + k] = sums[:16] + sums[16:]

    stream(NEAR_REST // REST_STEP, near_first, near_second)
    near_parts[NEAR_REST] = jnp.zeros((16, 128), F32)

    for copy in group_copies:
        copy.wait()
    for copy in loads[8:11]:
        copy.wait()

    def half_of(skel, start, which):
        tile = source_tile(skel, pl.multiple_of(start, 128), 128)
        at = row((8, 128))
        values = jnp.where(at == 0, tile[0], jnp.where(at == 1, tile[1], tile[2]))
        values = jnp.where(which == 0, values, pltpu.roll(values, 64, 1))
        return values.T[:64]

    def marked(links, base, count):
        at = lane((1, 64 * count)) // 64
        hit = at < 0
        for k in range(links.shape[1]):
            hit = hit | (at == links[0, k] - base)
        return hit.astype(F32)

    def small(target, skel, values, mark):
        kernel = pair_kernel(target, skel) * mark
        sums = dot(twice(jnp.concatenate(values, axis=1)), beside(kernel), NT)
        return sums[:16] + sums[16:]

    group_fields = small(
        half_of(group_skel_v, (g // 2) * 128, lax.rem(g, 2)),
        group_skel_v[...],
        in_pairs(groups, n_wide),
        marked(group_links, 0, n_wide),
    )
    node_fields = dot(group_fields, node_downward_v[...], NN, HIGH) + small(
        half_of(nodes_skel, (n // 2) * 128, lax.rem(n, 2)),
        nodes_skel[...],
        in_pairs(nodes, n_narrow),
        marked(node_links, g * n_narrow, n_narrow),
    )
    fields[...] = node_fields

    def collect(leaf, carry):
        span = pl.ds(pl.multiple_of(leaf * 128, 128), 128)
        value = near[:, span]
        for slot in range(1, near_list.shape[0]):
            value = value + near_parts[near_places[slot, leaf]]
        near[:, span] = value
        return carry

    lax.fori_loop(0, leaves, collect, 0, unroll=8)
    couple_store.wait()


def finish(fields, near, couple, leaf_downward, basis, out):
    field_halves = jnp.concatenate(halves(fields[...]), axis=0)
    low = lane((16, 128)) < 64
    for i in range(basis.shape[0]):
        at = slice(128 * i, 128 * (i + 1))
        product = dot(field_halves, beside(leaf_downward[:, at]), NN)
        leaf = product[:16, :128] + product[16:, :128] + product[:16, 128:] + couple[:, at]
        lefts = [jnp.where(low, leaf, 0.0), jnp.where(low, 0.0, leaf)]
        left = jnp.concatenate([h for x in lefts for h in halves(x)], axis=0)
        product = dot(left, beside(basis[i]), NN)
        for k in range(2):
            rows = product[32 * k : 32 * (k + 1)]
            span = slice(256 * i + 128 * k, 256 * i + 128 * (k + 1))
            out[:, span] = near[:, span] + (rows[:16, :128] + rows[16:, :128] + rows[:16, 128:])


def on_device(
    points,
    charges,
    leaf_skel,
    node_skel,
    group_skel,
    source_basis,
    target_basis,
    leaf_upward,
    leaf_downward,
    node_upward,
    node_downward,
    near_list,
    leaf_links,
    node_links,
    group_links,
):
    n_wide, n_narrow = lax.axis_size("wide"), lax.axis_size("narrow")
    leaves, rank, size = source_basis.shape
    vmem = pl.BlockSpec(memory_space=pltpu.VMEM)
    smem = pl.BlockSpec(memory_space=pltpu.SMEM)
    anywhere = pl.BlockSpec(memory_space=pl.ANY)
    tables = 3 * leaves + 1
    table = (16, 128)
    paired = (leaves // 2, 2 * rank, size)

    def f32(*shape):
        return pltpu.VMEM(shape, F32)

    def bf16(*shape):
        return pltpu.VMEM(shape, BF16)

    def sems(count):
        return pltpu.SemaphoreType.DMA((count,))

    near, couple, fields = pl.pallas_call(
        fused,
        out_shape=[
            jax.ShapeDtypeStruct(charges.shape, F32),
            jax.ShapeDtypeStruct((16, leaf_skel.shape[1]), F32),
            jax.ShapeDtypeStruct((16, rank), F32),
        ],
        in_specs=[anywhere] * 2 + [smem] * 2 + [anywhere] * 9,
        out_specs=[vmem, anywhere, vmem],
        scratch_shapes=[
            *[f32(*points.shape)] * 3,
            *[f32(*charges.shape)] * 3,
            *[f32(*leaf_skel.shape)] * 3,
            *[f32(16, leaf_skel.shape[1])] * 3,
            f32(*paired),
            f32(*leaf_upward.shape),
            f32(64, 64 * n_narrow),
            f32(6, 64 * n_narrow),
            f32(n_narrow, *table),
            f32(n_wide, *table),
            f32(*table),
            f32(*table),
            bf16(tables, 48, 256),
            bf16(tables, 32, 256),
            bf16(leaves, 128, 48),
            bf16(REST_STEP, 128, 256),
            f32(NEAR_REST + 1, *table),
            bf16(tables, 48, 256),
            bf16(tables, 32, 256),
            bf16(leaves, 64, 48),
            bf16(4 * FAR_STEP, 64, 256),
            pltpu.VMEM(near_list.shape[::-1], jnp.int32),
            pltpu.VMEM(leaf_links.shape[::-1], jnp.int32),
            f32(*group_skel.shape),
            f32(*node_downward.shape),
            f32(16, leaf_skel.shape[1]),
            pltpu.VMEM((1, 256), jnp.int32),
            pltpu.VMEM((8, 128), jnp.int32),
            pltpu.VMEM((8, 128), jnp.int32),
            pltpu.SMEM((1, 256), jnp.int32),
            pltpu.SMEM((8, 128), jnp.int32),
            pltpu.SMEM((8, 128), jnp.int32),
            sems(12),
            sems(3),
            sems(8),
            sems(8),
            sems(n_narrow),
            sems(n_narrow),
            sems(n_wide),
            sems(n_wide),
        ],
        compiler_params=pltpu.CompilerParams(
            collective_id=0, has_side_effects=True, vmem_limit_bytes=VMEM_LIMIT
        ),
        name="fused",
    )(
        near_list.T,
        leaf_links.T,
        node_links,
        group_links,
        points,
        charges,
        leaf_skel,
        source_basis.reshape(paired),
        leaf_upward,
        node_upward,
        node_skel,
        node_downward,
        group_skel,
    )
    steps = FINISH_STEPS

    def columns(rows, total):
        return pl.BlockSpec((rows, total // steps), lambda i: (0, i))

    return pl.pallas_call(
        finish,
        grid=(steps,),
        out_shape=jax.ShapeDtypeStruct(charges.shape, F32),
        in_specs=[
            pl.BlockSpec(fields.shape, lambda i: (0, 0)),
            columns(*near.shape),
            columns(*couple.shape),
            columns(*leaf_downward.shape),
            pl.BlockSpec((paired[0] // steps, *paired[1:]), lambda i: (i, 0, 0)),
        ],
        out_specs=columns(*near.shape),
        name="finish",
    )(fields, near, couple, leaf_downward, target_basis.reshape(paired))


def solution(mesh):
    both = ("wide", "narrow")
    in_specs = (
        P(None, both),
        P(None, both),
        P(None, both),
        P(),
        P(),
        P(both, None, None),
        P(both, None, None),
        P(None, both),
        P(None, both),
        P(),
        P(None, both),
        P(both, None),
        P(both, None),
        P(both, None),
        P("wide", None),
    )
    return jax.shard_map(
        on_device, mesh=mesh, in_specs=in_specs, out_specs=P(None, both), check_vma=False
    )
```
